256 devices in a mesh: ctx: 32 (over y, z), head: 8 (over x, core).
Axes of the slice: x: 4, y: 4, z: 8, core: 2. Of those that a mesh axis runs over, the one named last changes fastest.
Arguments:
- q_raw: bfloat16 [8192, 5120], P('ctx', 'head'), may hold values from -500 to 500
- k_raw: bfloat16 [8192, 5120], P('ctx', 'head'), may hold values from -500 to 500
- values: bfloat16 [8192, 5120], P('ctx', 'head'), may hold values from -6 to 6
- grad_out: bfloat16 [8192, 5120], P('ctx', 'head'), may hold values from -50 to 50
- gain_q: float32 [128], replicated, may hold values from 0.5 to 5
- gain_k: float32 [128], replicated, may hold values from 0.5 to 5
- pair_blocks: int32 [32, 2], P('ctx'), may hold values from 0 to 31, as said below
- pair_count: int32 [32], P('ctx'), may hold values from 0 to 2
Outputs:
- grad_q: bfloat16 [8192, 5120], P('ctx', 'head')
- grad_k: bfloat16 [8192, 5120], P('ctx', 'head')
- grad_v: bfloat16 [8192, 5120], P('ctx', 'head')
- grad_gain_q: float32 [128], replicated
- grad_gain_k: float32 [128], replicated
The draws below stay inside these ranges and needn't reach their ends.
Inputs may be any that keep to these rules, and one draw needn't show every extreme that they name: `pair_blocks`: row a lists each of the 2 blocks a XOR 2^i (i < 2) once, in some order. Its first pair_count[a] entries are the active partners of block a, each of them a XOR 2^i for an i at which bit i of a is 0: a pair is listed only at its lower block and is active in both directions.
All inputs are finite; a program needn't handle non-finite values.
Results may differ from the reference program's by a relative error of at most 0.015.
The reference program's roundings to bfloat16 on the way count: a program that leaves them out, or rounds other values in their place, can miss the bound.
Values may be sent and summed in bfloat16 or wider, within the bound.
A program may use at most 64 MiB of HBM per device.

```python
import math
import jax
import jax.numpy as jnp
from jax import lax

HEAD_DIM = 128
WIDTH = 5120
TOK_DEV = 256
BITS = 2
BLOCKS = 32
TOKENS = 8192


def marked_dims(key):
    order = jax.random.permutation(jax.random.fold_in(key, 500), HEAD_DIM)
    return order < 4


def pair_lists(key):
    key = jax.random.fold_in(key, 900)
    block_ids = jnp.arange(BLOCKS, dtype=jnp.int32)[:, None]
    bit_ids = jnp.arange(BITS, dtype=jnp.int32)[None, :]
    bit_masks = jnp.left_shift(jnp.int32(1), bit_ids)
    lower_side = jnp.bitwise_and(block_ids, bit_masks) == 0
    coins = jax.random.randint(jax.random.fold_in(key, 1), (BLOCKS, BITS), 0, 4)
    forced = (block_ids == 0) | (block_ids == BLOCKS - 2) | (block_ids == BLOCKS - 3)
    active = lower_side & ((coins > 0) | forced)
    ranks = jax.random.randint(jax.random.fold_in(key, 2), (BLOCKS, BITS), 0, 16)
    scores = jnp.where(active, 0, 64) + ranks * BITS + bit_ids
    order = jnp.argsort(scores, axis=1).astype(jnp.int32)
    partners = jnp.bitwise_xor(block_ids, jnp.left_shift(jnp.int32(1), order))
    counts = jnp.sum(active.astype(jnp.int32), axis=1)
    return (partners, counts)


def field_scales(key):
    column_key, row_key = jax.random.split(key)
    ramp = 1.0 + 2.0 * jnp.arange(WIDTH, dtype=jnp.float32) / max(WIDTH - 1, 1)
    columns = ramp * jnp.exp(jax.random.uniform(column_key, (WIDTH,), jnp.float32, 0.0, math.log(3.3)))
    row_scales = jnp.exp(jax.random.uniform(row_key, (TOKENS, 1), jnp.float32, 0.0, math.log(10.0)))
    return row_scales * columns[None, :]


def draw_q_raw(key, part):
    key = jax.random.fold_in(key, 3)
    scale_key, noise_key = jax.random.split(key, 2)
    scales = field_scales(scale_key)
    noise = jnp.clip(jax.random.normal(noise_key, (TOKENS, WIDTH), jnp.float32), -5.0, 5.0)
    return (scales * noise).astype(jnp.bfloat16)


def draw_k_raw(key, part):
    key = jax.random.fold_in(key, 4)
    scale_key, noise_key = jax.random.split(key, 2)
    scales = field_scales(scale_key)
    noise = jnp.clip(jax.random.normal(noise_key, (TOKENS, WIDTH), jnp.float32), -5.0, 5.0)
    return (scales * noise).astype(jnp.bfloat16)


def draw_grad_out(key, part):
    key = jax.random.fold_in(key, 5)
    column_key, noise_key = jax.random.split(key, 2)
    ramp = 1.0 + 2.0 * jnp.arange(TOKENS, dtype=jnp.float32)[:, None] / max(TOKENS - 1, 1)
    columns = jnp.exp(jax.random.uniform(column_key, (1, WIDTH), jnp.float32, 0.0, math.log(3.0)))
    noise = jnp.clip(jax.random.normal(noise_key, (TOKENS, WIDTH), jnp.float32), -5.0, 5.0)
    return (ramp * columns * noise).astype(jnp.bfloat16)


def draw_gain_q(key, part):
    marks = marked_dims(key)
    key = jax.random.fold_in(key, 1)
    drawn_key, large_key = jax.random.split(key)
    drawn = jnp.exp(jax.random.uniform(drawn_key, (HEAD_DIM,), jnp.float32, math.log(0.6), math.log(1.6)))
    large = jax.random.uniform(large_key, (HEAD_DIM,), jnp.float32, 1.8, 2.4)
    return jnp.where(marks, large, drawn).astype(jnp.float32)


def draw_gain_k(key, part):
    marks = marked_dims(key)
    key = jax.random.fold_in(key, 2)
    drawn_key, large_key = jax.random.split(key)
    drawn = jnp.exp(jax.random.uniform(drawn_key, (HEAD_DIM,), jnp.float32, math.log(0.6), math.log(1.6)))
    large = jax.random.uniform(large_key, (HEAD_DIM,), jnp.float32, 1.8, 2.4)
    return jnp.where(marks, large, drawn).astype(jnp.float32)


def draw_pair_blocks(key, part):
    partners, counts = pair_lists(key)
    return partners


def draw_pair_count(key, part):
    partners, counts = pair_lists(key)
    return counts


def steps_of(rng, dims, pieces, low, high):
    level = 1.0
    for position, blocks in pieces:
        heights = jax.random.uniform(jax.random.fold_in(jax.random.fold_in(rng, 6), position), (blocks,), jnp.float32, low / len(pieces), high / len(pieces))
        level = level * jnp.repeat(jnp.exp(heights), dims[position] // blocks).reshape((-1,) + (1,) * (len(dims) - 1 - position))
    return level


def centred(stream_key, dims, width, reach, shards=(), held_as=jnp.bfloat16):
    entries = jax.random.normal(stream_key, dims, jnp.float32) * width
    if len(shards) > 0:
        entries = steps_of(stream_key, dims, shards, -0.22, 0.18) * entries
    return jnp.clip(entries, min=-reach, max=reach).astype(held_as)


def setup_inputs(seed: int = 0) -> dict:
    streams_of = jax.random.split(jax.random.key(seed), 9)
    return {
        "q_raw": draw_q_raw(jax.random.fold_in(streams_of[8], 71), 0),
        "k_raw": draw_k_raw(jax.random.fold_in(streams_of[8], 71), 0),
        "values": centred(streams_of[2], (TOKENS, WIDTH), 1.0, 6.0, ((0, 32), (1, 8))),
        "grad_out": draw_grad_out(jax.random.fold_in(streams_of[8], 71), 0),
        "gain_q": draw_gain_q(jax.random.fold_in(streams_of[8], 71), 0),
        "gain_k": draw_gain_k(jax.random.fold_in(streams_of[8], 71), 0),
        "pair_blocks": draw_pair_blocks(jax.random.fold_in(streams_of[8], 71), 0),
        "pair_count": draw_pair_count(jax.random.fold_in(streams_of[8], 71), 0),
    }


FLOOR_LOG = -1e+30

def head_norm(raw_rows, gain):
    raw_float = raw_rows.astype(jnp.float32).reshape(raw_rows.shape[0], -1, HEAD_DIM)
    inverse = lax.rsqrt(lax.optimization_barrier(jnp.mean(raw_float * raw_float, axis=2, keepdims=True)) + 1e-06)
    return (raw_float, inverse, (raw_float * inverse * gain).astype(jnp.bfloat16))

def norm_back(raw_float, inverse, gain, grad_normed):
    gain_grad = gain * grad_normed
    inner = lax.optimization_barrier(jnp.sum(raw_float * gain_grad, axis=2, keepdims=True))
    return inverse * gain_grad - raw_float * inverse * inverse * inverse * inner / HEAD_DIM

def rounded(term):
    return lax.optimization_barrier(term.astype(jnp.bfloat16)).astype(jnp.float32)

def active_pairs(pair_blocks, pair_count):
    block_ids = jnp.arange(BLOCKS, dtype=jnp.int32)[:, None]
    bit_masks = jnp.left_shift(jnp.int32(1), jnp.arange(BITS, dtype=jnp.int32))[None, :]
    partners = jnp.bitwise_xor(block_ids, bit_masks)
    slot_live = jnp.arange(BITS, dtype=jnp.int32)[None, :] < pair_count[:, None]
    listed = jnp.any(slot_live[:, None, :] & (pair_blocks[:, None, :] == partners[:, :, None]), axis=2)
    lower_side = jnp.bitwise_and(block_ids, bit_masks) == 0
    from_lower = jnp.take_along_axis(listed, partners, axis=0)
    return jnp.where(lower_side, listed, from_lower)

def forward_part(query_rows, key_rows, value_rows, factor):
    scores = jnp.einsum('thd,shd->hts', query_rows.astype(jnp.float32), key_rows.astype(jnp.float32)) * factor
    largest = lax.optimization_barrier(jnp.max(scores, axis=2))
    log_total = largest + jnp.log(lax.optimization_barrier(jnp.sum(jnp.exp(scores - largest[:, :, None]), axis=2)))
    weights = jnp.exp(scores - log_total[:, :, None]).astype(jnp.bfloat16)
    partial_out = jnp.einsum('hts,shd->thd', weights.astype(jnp.float32), value_rows.astype(jnp.float32))
    return (log_total, partial_out)

def combine(log_parts, out_parts):
    stacked = jnp.stack(log_parts)
    largest = lax.optimization_barrier(jnp.max(stacked, axis=0))
    log_total = largest + jnp.log(lax.optimization_barrier(jnp.sum(jnp.exp(stacked - largest), axis=0)))
    merged = jnp.zeros_like(out_parts[0])
    for part_log, part_out in zip(log_parts, out_parts):
        merged = merged + jnp.exp(part_log - log_total).T[:, :, None] * part_out
    return (log_total, merged)

def query_side(query_rows, key_rows, value_rows, grad_rows, log_total, row_dot, factor):
    scores = jnp.einsum('thd,shd->hts', query_rows.astype(jnp.float32), key_rows.astype(jnp.float32)) * factor
    weights = jnp.exp(scores - log_total[:, :, None])
    grad_prob = jnp.einsum('thd,shd->hts', grad_rows.astype(jnp.float32), value_rows.astype(jnp.float32))
    grad_score = (weights * (grad_prob - row_dot[:, :, None]) * factor).astype(jnp.bfloat16)
    return jnp.einsum('hts,shd->thd', grad_score.astype(jnp.float32), key_rows.astype(jnp.float32))

def key_side(query_rows, key_rows, value_rows, grad_rows, log_total, row_dot, factor):
    scores = jnp.einsum('thd,shd->hts', query_rows.astype(jnp.float32), key_rows.astype(jnp.float32)) * factor
    weights = jnp.exp(scores - log_total[:, :, None])
    weights_low = weights.astype(jnp.bfloat16)
    grad_value = jnp.einsum('hts,thd->shd', weights_low.astype(jnp.float32), grad_rows.astype(jnp.float32))
    grad_prob = jnp.einsum('thd,shd->hts', grad_rows.astype(jnp.float32), value_rows.astype(jnp.float32))
    grad_score = (weights * (grad_prob - row_dot[:, :, None]) * factor).astype(jnp.bfloat16)
    grad_key = jnp.einsum('hts,thd->shd', grad_score.astype(jnp.float32), query_rows.astype(jnp.float32))
    return (grad_key, grad_value)

def reference(q_raw, k_raw, values, grad_out, gain_q, gain_k, pair_blocks, pair_count):
    factor = 1.0 / math.sqrt(HEAD_DIM)
    q_float, q_inverse, query = head_norm(q_raw, gain_q)
    k_float, k_inverse, key_all = head_norm(k_raw, gain_k)
    heads_all = query.shape[1]
    block_shape = (BLOCKS, TOK_DEV, heads_all, HEAD_DIM)
    query_blocks = query.reshape(block_shape)
    key_blocks = key_all.reshape(block_shape)
    value_blocks = values.reshape(block_shape)
    grad_blocks = grad_out.reshape(block_shape)
    active = active_pairs(pair_blocks, pair_count)

    def forward_block(block):
        query_here = query_blocks[block]
        first_log, first_out = forward_part(query_here, key_blocks[block], value_blocks[block], factor)
        log_parts = [first_log]
        out_parts = [first_out]
        for bit_index in range(BITS):
            partner = jnp.bitwise_xor(block, 1 << bit_index)
            part_log, part_out = forward_part(query_here, key_blocks[partner], value_blocks[partner], factor)
            log_parts.append(jnp.where(active[block, bit_index], part_log, FLOOR_LOG))
            out_parts.append(part_out)
        log_total, merged = combine(log_parts, out_parts)
        row_dot = lax.optimization_barrier(jnp.sum(grad_blocks[block].astype(jnp.float32) * merged, axis=2)).T
        return (log_total, row_dot)
    block_ids = jnp.arange(BLOCKS, dtype=jnp.int32)
    log_all, dot_all = lax.map(forward_block, block_ids)

    def backward_block(block):
        query_here = query_blocks[block]
        key_here = key_blocks[block]
        value_here = value_blocks[block]
        grad_here = grad_blocks[block]
        grad_q_sum = query_side(query_here, key_here, value_here, grad_here, log_all[block], dot_all[block], factor)
        grad_k_sum, grad_v_sum = key_side(query_here, key_here, value_here, grad_here, log_all[block], dot_all[block], factor)
        for bit_index in range(BITS):
            partner = jnp.bitwise_xor(block, 1 << bit_index)
            flag = active[block, bit_index].astype(jnp.float32)
            near_q = query_side(query_here, key_blocks[partner], value_blocks[partner], grad_here, log_all[block], dot_all[block], factor)
            near_k, near_v = key_side(query_blocks[partner], key_here, value_here, grad_blocks[partner], log_all[partner], dot_all[partner], factor)
            grad_q_sum = grad_q_sum + flag * rounded(near_q)
            grad_k_sum = grad_k_sum + flag * rounded(near_k)
            grad_v_sum = grad_v_sum + flag * rounded(near_v)
        return (grad_q_sum, grad_k_sum, grad_v_sum)
    grad_q_blocks, grad_k_blocks, grad_v_blocks = lax.map(backward_block, block_ids)
    grad_shape = (TOKENS, heads_all, HEAD_DIM)
    grad_q_normed = grad_q_blocks.reshape(grad_shape)
    grad_k_normed = grad_k_blocks.reshape(grad_shape)
    grad_q = norm_back(q_float, q_inverse, gain_q, grad_q_normed).reshape(TOKENS, -1).astype(jnp.bfloat16)
    grad_k = norm_back(k_float, k_inverse, gain_k, grad_k_normed).reshape(TOKENS, -1).astype(jnp.bfloat16)
    grad_v = grad_v_blocks.reshape(TOKENS, -1).astype(jnp.bfloat16)
    grad_gain_q = lax.optimization_barrier(jnp.sum(grad_q_normed * q_float * q_inverse, axis=(0, 1)))
    grad_gain_k = lax.optimization_barrier(jnp.sum(grad_k_normed * k_float * k_inverse, axis=(0, 1)))
    return (grad_q, grad_k, grad_v, grad_gain_q, grad_gain_k)
```

```python
import math

import jax
import jax.numpy as jnp
from jax import lax
from jax.experimental import pallas as pl
from jax.experimental.pallas import tpu as pltpu
from jax.sharding import PartitionSpec as P

HEAD_DIM = 128
BITS = 2
ROWS = 256
HEADS = 5
FLOOR_LOG = -1e30
FACTOR = 1.0 / math.sqrt(HEAD_DIM)
LOG2E = 1.0 / math.log(2.0)
HEAD_DEVS = 8
Y_DEVS = 4
Z_DEVS = 8
PEERS = (HEAD_DEVS - 1) + (Y_DEVS - 1) + (Z_DEVS - 1)
MESH = pl.DeviceIdType.MESH
NT = (((1,), (1,)), ((), ()))
NN = (((1,), (0,)), ((), ()))
TN = (((0,), (0,)), ((), ()))


def mm(a, b, dims):
    return lax.dot_general(a, b, dims, preferred_element_type=jnp.float32)


def kernel(
    q_hbm, k_hbm, v_hbm, g_hbm, gain_q_ref, gain_k_ref, blocks_ref, count_ref,
    oq_hbm, ok_hbm, ov_hbm, ogain_q_ref, ogain_k_ref,
    raw_q, raw_k, qn, kn, vn, gn, rq, rg,
    q_hat, q_inv, k_hat, k_inv, prob, dprob, stat_own, stat_out, stat_in,
    fin_own, fin_out, fin_in, dq_own, dq_out, dq_in, oq, ok, ov, acc,
    sum_a, sum_b, sum_c,
    load_sem, store_sem, qs, qr, gs, gr, ss, sr, fs, fr, ds, dr, as_, ar,
):
    place = lax.axis_index("ctx")
    column = lax.axis_index("head")
    z = lax.rem(place, Z_DEVS)
    y = lax.div(place, Z_DEVS)
    partners = [jnp.bitwise_xor(place, 1 << i) for i in range(BITS)]
    lower = [jnp.bitwise_and(place, 1 << i) == 0 for i in range(BITS)]

    head_peers = [{"head": lax.rem(column + r, HEAD_DEVS)} for r in range(1, HEAD_DEVS)]
    y_peers = [{"ctx": lax.rem(y + r, Y_DEVS) * Z_DEVS + z} for r in range(1, Y_DEVS)]
    z_peers = [{"ctx": y * Z_DEVS + lax.rem(z + r, Z_DEVS)} for r in range(1, Z_DEVS)]

    barrier = pltpu.get_barrier_semaphore()
    for peer in z_peers + y_peers + head_peers:
        pl.semaphore_signal(barrier, 1, device_id=peer, device_id_type=MESH)

    def load(src, dst, slot, h):
        return pltpu.make_async_copy(
            src.at[:, h * HEAD_DIM : (h + 1) * HEAD_DIM], dst.at[h], load_sem.at[slot, h]
        )

    sources = ((g_hbm, gn), (q_hbm, raw_q), (k_hbm, raw_k), (v_hbm, vn))
    for slot, (src, dst) in enumerate(sources):
        for h in range(HEADS):
            load(src, dst, slot, h).start()

    def remote(src, dst, send, recv, peer):
        return pltpu.make_async_remote_copy(
            src_ref=src, dst_ref=dst, send_sem=send, recv_sem=recv,
            device_id=peer, device_id_type=MESH,
        )

    def q_copy(h, i):
        return remote(qn.at[h], rq.at[i, h], qs.at[i, h], qr.at[i, h], {"ctx": partners[i]})

    def g_copy(h, i):
        return remote(gn.at[h], rg.at[i, h], gs.at[i, h], gr.at[i, h], {"ctx": partners[i]})

    def s_copy(h, i):
        return remote(stat_out.at[i, h], stat_in.at[i, h], ss.at[i, h], sr.at[i, h], {"ctx": partners[i]})

    def f_copy(h, i):
        return remote(fin_out.at[i, h], fin_in.at[i, h], fs.at[i, h], fr.at[i, h], {"ctx": partners[i]})

    def d_copy(h, i):
        return remote(dq_out.at[i, h], dq_in.at[i, h], ds.at[i, h], dr.at[i, h], {"ctx": partners[i]})

    listed = []
    for i in range(BITS):
        hit = jnp.float32(0.0)
        for slot in range(BITS):
            live = (blocks_ref[0, slot] == partners[i]) & (slot < count_ref[0])
            hit = jnp.where(live, 1.0, hit)
        listed.append(hit)
    off = [jnp.where(lower[i], 1.0 - listed[i], 0.0) for i in range(BITS)]

    gain_q = gain_q_ref[...]
    gain_k = gain_k_ref[...]

    def norm(raw, gain, hat, inv, normed, h):
        x = raw[h].astype(jnp.float32)
        inverse = lax.rsqrt(jnp.mean(x * x, axis=1, keepdims=True) + 1e-06)
        x_hat = x * inverse
        hat[h] = x_hat
        inv[h] = jnp.broadcast_to(inverse, x.shape)
        normed[h] = (x_hat * gain).astype(jnp.bfloat16)

    for h in range(HEADS):
        load(q_hbm, raw_q, 1, h).wait()
        load(g_hbm, gn, 0, h).wait()
        norm(raw_q, gain_q, q_hat, q_inv, qn, h)
        if h == 0:
            pl.semaphore_wait(barrier, PEERS)
        for i in (1, 0):
            g_copy(h, i).start()
            q_copy(h, i).start()
    for h in range(HEADS):
        load(k_hbm, raw_k, 2, h).wait()
        load(v_hbm, vn, 3, h).wait()
        norm(raw_k, gain_k, k_hat, k_inv, kn, h)
    acc[...] = jnp.zeros_like(acc)

    def forward(h, slot, query, grad):
        scores = mm(kn[h], query, NT)
        largest = jnp.max(scores, axis=0, keepdims=True)
        e = jnp.exp2((scores - largest) * (FACTOR * LOG2E))
        total = jnp.sum(e, axis=0, keepdims=True)
        p = e * (1.0 / total)
        dp = mm(vn[h], grad, NT)
        prob[slot, h] = p
        dprob[slot, h] = dp
        dot = jnp.sum(p.astype(jnp.bfloat16).astype(jnp.float32) * dp, axis=0, keepdims=True)
        return largest * FACTOR + jnp.log(total), dot

    def far_forward(h):
        for i in (0, 1):
            g_copy(h, i).wait_recv()
            q_copy(h, i).wait_recv()
            log, dot = forward(h, i + 1, rq[i, h], rg[i, h])
            stat_out[i, h, 0:1] = jnp.where(off[i] > 0.5, FLOOR_LOG, log)
            stat_out[i, h, 1:2] = dot
            s_copy(h, i).start()

    def near_forward(h):
        log, dot = forward(h, 0, qn[h], gn[h])
        stat_own[h, 0:1] = log
        stat_own[h, 1:2] = dot

    def combine(h):
        logs = [stat_own[h, 0:1]]
        dots = [stat_own[h, 1:2]]
        for i in range(BITS):
            s_copy(h, i).wait_recv()
            logs.append(jnp.where(off[i] > 0.5, FLOOR_LOG, stat_in[i, h, 0:1]))
            dots.append(stat_in[i, h, 1:2])
        top = jnp.maximum(jnp.maximum(logs[0], logs[1]), logs[2])
        parts = [jnp.exp(log - top) for log in logs]
        inverse = 1.0 / (parts[0] + parts[1] + parts[2])
        shares = [part * inverse for part in parts]
        row_dot = shares[0] * dots[0] + shares[1] * dots[1] + shares[2] * dots[2]
        for i in range(BITS):
            fin_out[i, h, 0:1] = shares[i + 1]
            fin_out[i, h, 1:2] = row_dot
            f_copy(h, i).start()
        fin_own[h, 0:1] = shares[0]
        fin_own[h, 1:2] = row_dot

    def one_back(h, slot, query, grad, share, row_dot):
        w = prob[slot, h] * share
        ds_t = (w * (dprob[slot, h] - row_dot) * FACTOR).astype(jnp.bfloat16)
        dv = mm(w.astype(jnp.bfloat16), grad, NN)
        dk = mm(ds_t, query, NN)
        dq = mm(ds_t, kn[h], TN)
        return dq, dk, dv

    def norm_back(hat, inv, gain, grad):
        gg = grad * gain
        inner = jnp.mean(hat * gg, axis=1, keepdims=True)
        return (inv * (gg - hat * inner)).astype(jnp.bfloat16)

    def fold(a):
        return jnp.sum(a.reshape(ROWS // 8, 8, HEAD_DIM), axis=0)

    def columns(h):
        return pl.ds(pl.multiple_of(h * HEAD_DIM, HEAD_DIM), HEAD_DIM)

    def store(src, dst, slot, h):
        return pltpu.make_async_copy(src.at[h], dst.at[:, columns(h)], store_sem.at[slot, h])

    def backward(h):
        for i in range(BITS):
            f_copy(h, i).wait_recv()
            dq, dk, dv = one_back(
                h, i + 1, rq[i, h], rg[i, h], fin_in[i, h, 0:1], fin_in[i, h, 1:2]
            )
            dq_out[i, h] = dq.astype(jnp.bfloat16)
            d_copy(h, i).start()
            acc[1] += fold(dq * rq[i, h].astype(jnp.float32))
            if i == 0:
                gk, gv = dk, dv
            else:
                gk, gv = gk + dk, gv + dv
        dq, dk, dv = one_back(h, 0, qn[h], gn[h], fin_own[h, 0:1], fin_own[h, 1:2])
        gk, gv = gk + dk, gv + dv
        dq_own[h] = dq
        acc[0] += fold(dq * q_hat[h])
        acc[2] += fold(gk * k_hat[h])
        ov[h] = gv.astype(jnp.bfloat16)
        store(ov, ov_hbm, 2, h).start()
        ok[h] = norm_back(k_hat[h], k_inv[h], gain_k, gk)
        store(ok, ok_hbm, 1, h).start()

    def step(h, carry):
        @pl.when(h < HEADS)
        def _():
            far_forward(h)
            near_forward(h)
            combine(h)

        @pl.when(h > 0)
        def _():
            backward(h - 1)

        return carry

    lax.fori_loop(0, HEADS + 1, step, 0)

    def finish(h):
        for i in range(BITS):
            d_copy(h, i).wait_recv()
        gq = dq_own[h] + dq_in[0, h].astype(jnp.float32) + dq_in[1, h].astype(jnp.float32)
        oq[h] = norm_back(q_hat[h], q_inv[h], gain_q, gq)
        store(oq, oq_hbm, 0, h).start()

    def share_copies(buffer, index, peers, base):
        return [
            remote(buffer.at[index], buffer.at[index], as_.at[base + r], ar.at[base + r], peer)
            for r, peer in enumerate(peers)
        ]

    copies_a = share_copies(sum_a, column, head_peers, 0)
    copies_b = share_copies(sum_b, y, y_peers, HEAD_DEVS - 1)
    copies_c = share_copies(sum_c, z, z_peers, HEAD_DEVS + Y_DEVS - 2)

    part_q = jnp.sum(acc[0], axis=0, keepdims=True) + jnp.sum(acc[1], axis=0, keepdims=True) / gain_q
    sum_a[column, 0:1] = part_q
    sum_a[column, 1:2] = jnp.sum(acc[2], axis=0, keepdims=True)
    for c in copies_a:
        c.start()
    finish(0)
    finish(1)
    for c in copies_a:
        c.wait_recv()
    sum_b[y] = jnp.sum(sum_a[...], axis=0)
    for c in copies_b:
        c.start()
    finish(2)
    for c in copies_b:
        c.wait_recv()
    sum_c[z] = jnp.sum(sum_b[...], axis=0)
    for c in copies_c:
        c.start()
    finish(3)
    finish(4)
    for c in copies_c:
        c.wait_recv()
    total = jnp.sum(sum_c[...], axis=0)
    ogain_q_ref[...] = total[0:1]
    ogain_k_ref[...] = total[1:2]

    for c in copies_a + copies_b + copies_c:
        c.wait_send()
    for h in range(HEADS):
        for i in range(BITS):
            q_copy(h, i).wait_send()
            g_copy(h, i).wait_send()
            s_copy(h, i).wait_send()
            f_copy(h, i).wait_send()
            d_copy(h, i).wait_send()
        for slot, (src, dst) in enumerate(((oq, oq_hbm), (ok, ok_hbm), (ov, ov_hbm))):
            store(src, dst, slot, h).wait()


def body(q_raw, k_raw, values, grad_out, gain_q, gain_k, pair_blocks, pair_count):
    def vmem(*shape, dtype=jnp.float32):
        return pltpu.VMEM(shape, dtype)

    low = jnp.bfloat16
    tile = (HEADS, ROWS, HEAD_DIM)
    square = (BITS + 1, HEADS, ROWS, ROWS)
    wide = jax.ShapeDtypeStruct((ROWS, HEADS * HEAD_DIM), low)
    narrow = jax.ShapeDtypeStruct((1, HEAD_DIM), jnp.float32)
    any_space = pl.BlockSpec(memory_space=pl.ANY)
    in_vmem = pl.BlockSpec(memory_space=pltpu.VMEM)
    in_smem = pl.BlockSpec(memory_space=pltpu.SMEM)
    pair = pltpu.SemaphoreType.DMA((BITS, HEADS))
    grad_q, grad_k, grad_v, sum_q, sum_k = pl.pallas_call(
        kernel,
        out_shape=(wide, wide, wide, narrow, narrow),
        in_specs=[any_space] * 4 + [in_vmem] * 2 + [in_smem] * 2,
        out_specs=(any_space, any_space, any_space, in_vmem, in_vmem),
        scratch_shapes=[
            vmem(*tile, dtype=low), vmem(*tile, dtype=low),
            vmem(*tile, dtype=low), vmem(*tile, dtype=low), vmem(*tile, dtype=low), vmem(*tile, dtype=low),
            vmem(BITS, *tile, dtype=low), vmem(BITS, *tile, dtype=low),
            vmem(*tile), vmem(*tile), vmem(*tile), vmem(*tile),
            vmem(*square), vmem(*square),
            vmem(HEADS, 2, ROWS), vmem(BITS, HEADS, 2, ROWS), vmem(BITS, HEADS, 2, ROWS),
            vmem(HEADS, 2, ROWS), vmem(BITS, HEADS, 2, ROWS), vmem(BITS, HEADS, 2, ROWS),
            vmem(*tile), vmem(BITS, *tile, dtype=low), vmem(BITS, *tile, dtype=low),
            vmem(*tile, dtype=low), vmem(*tile, dtype=low), vmem(*tile, dtype=low),
            vmem(3, 8, HEAD_DIM),
            vmem(HEAD_DEVS, 2, HEAD_DIM), vmem(Y_DEVS, 2, HEAD_DIM), vmem(Z_DEVS, 2, HEAD_DIM),
            pltpu.SemaphoreType.DMA((4, HEADS)), pltpu.SemaphoreType.DMA((3, HEADS)),
            pair, pair, pair, pair, pair, pair, pair, pair, pair, pair,
            pltpu.SemaphoreType.DMA((PEERS,)), pltpu.SemaphoreType.DMA((PEERS,)),
        ],
        compiler_params=pltpu.CompilerParams(
            collective_id=0, has_side_effects=True, vmem_limit_bytes=40 * 1024 * 1024
        ),
        cost_estimate=pl.CostEstimate(
            flops=2 * 5 * 15 * ROWS * ROWS * HEAD_DIM,
            bytes_accessed=7 * ROWS * HEADS * HEAD_DIM * 2,
            transcendentals=15 * ROWS * ROWS,
        ),
    )(
        q_raw, k_raw, values, grad_out,
        gain_q.reshape(1, HEAD_DIM), gain_k.reshape(1, HEAD_DIM), pair_blocks, pair_count,
    )
    return grad_q, grad_k, grad_v, sum_q.reshape(HEAD_DIM), sum_k.reshape(HEAD_DIM)


def solution(mesh):
    placed = (
        P("ctx", "head"),
        P("ctx", "head"),
        P("ctx", "head"),
        P("ctx", "head"),
        P(),
        P(),
        P("ctx", None),
        P("ctx"),
    )
    return jax.shard_map(
        body,
        mesh=mesh,
        in_specs=placed,
        out_specs=(P("ctx", "head"), P("ctx", "head"), P("ctx", "head"), P(), P()),
        check_vma=False,
    )
```

```python
import math

import jax
import jax.numpy as jnp
from jax import lax
from jax.experimental import pallas as pl
from jax.experimental.pallas import tpu as pltpu
from jax.sharding import PartitionSpec as P

HEAD_DIM = 128
BITS = 2
ROWS = 256
HEADS = 5
FLOOR_LOG = -1e30
FACTOR = 1.0 / math.sqrt(HEAD_DIM)
LOG2E = 1.0 / math.log(2.0)
HEAD_DEVS = 8
Y_DEVS = 4
Z_DEVS = 8
PEERS = (HEAD_DEVS - 1) + (Y_DEVS - 1) + (Z_DEVS - 1)
MESH = pl.DeviceIdType.MESH
ORDER = (
    "N0 Q0 N1 Q1 " "N2 N3 N4 K0 " "K1 K2 K3 K4 " "L0 L1 L2 L3 " "L4 F0 Q2 F1 " "C0 Q3 G0 F2 " "C1 Q4 G1 F3 " "C2 G2 B0 D0 " "H0 F4 C3 G3 " "B1 D1 H1 C4 " "G4 B2 D2 B3 " "B4 A0 D3 H2 " "H3 H4 E0 A1 " "D4 E1 W0 W1 " "A2 E2 W2 E3 " "W3 E4 W4 A3 "
)
NT = (((1,), (1,)), ((), ()))
NN = (((1,), (0,)), ((), ()))
TN = (((0,), (0,)), ((), ()))


def mm(a, b, dims):
    return lax.dot_general(a, b, dims, preferred_element_type=jnp.float32)


def kernel(
    q_hbm, k_hbm, v_hbm, g_hbm, gain_q_ref, gain_k_ref, blocks_ref, count_ref,
    oq_hbm, ok_hbm, ov_hbm, ogain_ref,
    raw_q, raw_k, qn, kn, vn, gn, rq, rg,
    q_hat, q_inv, k_hat, k_inv, prob, dprob, stat_own, stat_out, stat_in,
    fin_own, fin_out, fin_in, dq_own, dk_sum, dv_sum, dq_out, dq_in, oq, ok, ov, acc,
    sum_a, sum_b, sum_c,
    load_sem, store_sem, qs, qr, gs, gr, ss, sr, fs, fr, ds, dr, as_, ar,
):
    place = lax.axis_index("ctx")
    column = lax.axis_index("head")
    z = lax.rem(place, Z_DEVS)
    y = lax.div(place, Z_DEVS)
    partners = [jnp.bitwise_xor(place, 1 << i) for i in range(BITS)]
    lower = [jnp.bitwise_and(place, 1 << i) == 0 for i in range(BITS)]

    head_peers = [{"head": lax.rem(column + r, HEAD_DEVS)} for r in range(1, HEAD_DEVS)]
    y_peers = [{"ctx": lax.rem(y + r, Y_DEVS) * Z_DEVS + z} for r in range(1, Y_DEVS)]
    z_peers = [{"ctx": y * Z_DEVS + lax.rem(z + r, Z_DEVS)} for r in range(1, Z_DEVS)]

    barrier = pltpu.get_barrier_semaphore()
    for peer in z_peers + y_peers + head_peers:
        pl.semaphore_signal(barrier, 1, device_id=peer, device_id_type=MESH)

    def load(src, dst, slot, h):
        return pltpu.make_async_copy(
            src.at[:, h * HEAD_DIM : (h + 1) * HEAD_DIM], dst.at[h], load_sem.at[slot, h]
        )

    sources = ((g_hbm, gn), (q_hbm, raw_q), (k_hbm, raw_k), (v_hbm, vn))
    for slot, (src, dst) in enumerate(sources):
        for h in range(HEADS):
            load(src, dst, slot, h).start()

    def remote(src, dst, send, recv, peer):
        return pltpu.make_async_remote_copy(
            src_ref=src, dst_ref=dst, send_sem=send, recv_sem=recv,
            device_id=peer, device_id_type=MESH,
        )

    def q_copy(h, i):
        return remote(qn.at[h], rq.at[i, h], qs.at[i, h], qr.at[i, h], {"ctx": partners[i]})

    def g_copy(h, i):
        return remote(gn.at[h], rg.at[i, h], gs.at[i, h], gr.at[i, h], {"ctx": partners[i]})

    def s_copy(h, i):
        return remote(stat_out.at[i, h], stat_in.at[i, h], ss.at[i, h], sr.at[i, h], {"ctx": partners[i]})

    def f_copy(h, i):
        return remote(fin_out.at[i, h], fin_in.at[i, h], fs.at[i, h], fr.at[i, h], {"ctx": partners[i]})

    def d_copy(h, i):
        return remote(dq_out.at[i, h], dq_in.at[i, h], ds.at[i, h], dr.at[i, h], {"ctx": partners[i]})

    listed = []
    for i in range(BITS):
        hit = jnp.float32(0.0)
        for slot in range(BITS):
            live = (blocks_ref[0, slot] == partners[i]) & (slot < count_ref[0])
            hit = jnp.where(live, 1.0, hit)
        listed.append(hit)
    off = [jnp.where(lower[i], 1.0 - listed[i], 0.0) for i in range(BITS)]

    gain_q = gain_q_ref[...]
    gain_k = gain_k_ref[...]

    def norm(raw, gain, hat, inv, normed, h):
        x = raw[h].astype(jnp.float32)
        inverse = lax.rsqrt(jnp.mean(x * x, axis=1, keepdims=True) + 1e-06)
        x_hat = x * inverse
        hat[h] = x_hat
        inv[h] = jnp.broadcast_to(inverse, x.shape)
        normed[h] = (x_hat * gain).astype(jnp.bfloat16)

    def norm_query(h):
        load(q_hbm, raw_q, 1, h).wait()
        load(g_hbm, gn, 0, h).wait()
        norm(raw_q, gain_q, q_hat, q_inv, qn, h)

    def send(h):
        if h == 0:
            pl.semaphore_wait(barrier, PEERS)
        for i in (1, 0):
            g_copy(h, i).start()
            q_copy(h, i).start()

    def norm_key(h):
        load(k_hbm, raw_k, 2, h).wait()
        load(v_hbm, vn, 3, h).wait()
        norm(raw_k, gain_k, k_hat, k_inv, kn, h)

    acc[...] = jnp.zeros_like(acc)

    def forward(h, slot, query, grad):
        scores = mm(kn[h], query, NT)
        largest = jnp.max(scores, axis=0, keepdims=True)
        e = jnp.exp2((scores - largest) * (FACTOR * LOG2E))
        total = jnp.sum(e, axis=0, keepdims=True)
        p = e * (1.0 / total)
        dp = mm(vn[h], grad, NT)
        prob[slot, h] = p
        dprob[slot, h] = dp
        dot = jnp.sum(p.astype(jnp.bfloat16).astype(jnp.float32) * dp, axis=0, keepdims=True)
        return largest * FACTOR + jnp.log(total), dot

    def far_forward(h):
        for i in (0, 1):
            g_copy(h, i).wait_recv()
            q_copy(h, i).wait_recv()
            log, dot = forward(h, i + 1, rq[i, h], rg[i, h])
            stat_out[i, h, 0:1] = jnp.where(off[i] > 0.5, FLOOR_LOG, log)
            stat_out[i, h, 1:2] = dot
            s_copy(h, i).start()

    def near_forward(h):
        log, dot = forward(h, 0, qn[h], gn[h])
        stat_own[h, 0:1] = log
        stat_own[h, 1:2] = dot

    def combine(h):
        logs = [stat_own[h, 0:1]]
        dots = [stat_own[h, 1:2]]
        for i in range(BITS):
            s_copy(h, i).wait_recv()
            logs.append(jnp.where(off[i] > 0.5, FLOOR_LOG, stat_in[i, h, 0:1]))
            dots.append(stat_in[i, h, 1:2])
        top = jnp.maximum(jnp.maximum(logs[0], logs[1]), logs[2])
        parts = [jnp.exp(log - top) for log in logs]
        inverse = 1.0 / (parts[0] + parts[1] + parts[2])
        shares = [part * inverse for part in parts]
        row_dot = shares[0] * dots[0] + shares[1] * dots[1] + shares[2] * dots[2]
        for i in range(BITS):
            fin_out[i, h, 0:1] = shares[i + 1]
            fin_out[i, h, 1:2] = row_dot
            f_copy(h, i).start()
        fin_own[h, 0:1] = shares[0]
        fin_own[h, 1:2] = row_dot

    def one_back(h, slot, query, grad, share, row_dot):
        w = prob[slot, h] * share
        ds_t = (w * (dprob[slot, h] - row_dot) * FACTOR).astype(jnp.bfloat16)
        dv = mm(w.astype(jnp.bfloat16), grad, NN)
        dk = mm(ds_t, query, NN)
        dq = mm(ds_t, kn[h], TN)
        return dq, dk, dv

    def norm_back(hat, inv, gain, grad):
        gg = grad * gain
        inner = jnp.mean(hat * gg, axis=1, keepdims=True)
        return (inv * (gg - hat * inner)).astype(jnp.bfloat16)

    def fold(a):
        return jnp.sum(a.reshape(ROWS // 8, 8, HEAD_DIM), axis=0)

    def columns(h):
        return slice(h * HEAD_DIM, (h + 1) * HEAD_DIM)

    def store(src, dst, slot, h):
        return pltpu.make_async_copy(src.at[h], dst.at[:, columns(h)], store_sem.at[slot, h])

    def near_back(h):
        dq, dk, dv = one_back(h, 0, qn[h], gn[h], fin_own[h, 0:1], fin_own[h, 1:2])
        dq_own[h] = dq
        dk_sum[h] = dk
        dv_sum[h] = dv
        acc[0] += fold(dq * q_hat[h])

    def far_back(h):
        gk, gv = dk_sum[h], dv_sum[h]
        for i in (1, 0):
            f_copy(h, i).wait_recv()
            dq, dk, dv = one_back(
                h, i + 1, rq[i, h], rg[i, h], fin_in[i, h, 0:1], fin_in[i, h, 1:2]
            )
            dq_out[i, h] = dq.astype(jnp.bfloat16)
            acc[1] += fold(dq * rq[i, h].astype(jnp.float32))
            gk, gv = gk + dk, gv + dv
        dk_sum[h] = gk
        dv_sum[h] = gv
        acc[2] += fold(gk * k_hat[h])

    def write_kv(h):
        ov[h] = dv_sum[h].astype(jnp.bfloat16)
        store(ov, ov_hbm, 2, h).start()
        ok[h] = norm_back(k_hat[h], k_inv[h], gain_k, dk_sum[h])
        store(ok, ok_hbm, 1, h).start()

    def send_dq(h):
        for i in (1, 0):
            d_copy(h, i).start()

    def finish(h):
        for i in range(BITS):
            d_copy(h, i).wait_recv()
        gq = dq_own[h] + dq_in[0, h].astype(jnp.float32) + dq_in[1, h].astype(jnp.float32)
        oq[h] = norm_back(q_hat[h], q_inv[h], gain_q, gq)
        store(oq, oq_hbm, 0, h).start()

    def share_copies(buffer, index, peers, base):
        return [
            remote(buffer.at[index], buffer.at[index], as_.at[base + r], ar.at[base + r], peer)
            for r, peer in enumerate(peers)
        ]

    copies_a = share_copies(sum_a, column, head_peers, 0)
    copies_b = share_copies(sum_b, y, y_peers, HEAD_DEVS - 1)
    copies_c = share_copies(sum_c, z, z_peers, HEAD_DEVS + Y_DEVS - 2)

    def gain_sums(stage):
        if stage == 0:
            part_q = jnp.sum(acc[0], axis=0, keepdims=True)
            part_q += jnp.sum(acc[1], axis=0, keepdims=True) / gain_q
            sum_a[column, 0:1] = part_q
            sum_a[column, 1:2] = jnp.sum(acc[2], axis=0, keepdims=True)
            for c in copies_a:
                c.start()
        elif stage == 1:
            for c in copies_a:
                c.wait_recv()
            sum_b[y] = jnp.sum(sum_a[...], axis=0)
            for c in copies_b:
                c.start()
        elif stage == 2:
            for c in copies_a:
                c.wait_send()
            for c in copies_b:
                c.wait_recv()
            sum_c[z] = jnp.sum(sum_b[...], axis=0)
            for c in copies_c:
                c.start()
        else:
            for c in copies_b:
                c.wait_send()
            for c in copies_c:
                c.wait_recv()
            total = jnp.sum(sum_c[...], axis=0)
            ogain_ref[...] = total

    def wait_sent(h):
        for i in range(BITS):
            for copy in (q_copy, g_copy, s_copy, f_copy, d_copy):
                copy(h, i).wait_send()
        for slot, (src, dst) in enumerate(((oq, oq_hbm), (ok, ok_hbm), (ov, ov_hbm))):
            store(src, dst, slot, h).wait()

    steps = {
        "N": norm_query, "Q": send, "K": norm_key, "L": near_forward, "F": far_forward,
        "C": combine, "G": near_back, "B": far_back, "H": write_kv, "W": wait_sent, "D": send_dq, "E": finish, "A": gain_sums,
    }
    for word in ORDER.split():
        steps[word[0]](int(word[1]))

    for c in copies_c:
        c.wait_send()


def hand_over(q, k, v, gains, oq, ok, ov, ogain_q, ogain_k, sem):
    pairs = ((q, oq), (k, ok), (v, ov), (gains.at[0:1], ogain_q), (gains.at[1:2], ogain_k))
    copies = [pltpu.make_async_copy(src, dst, sem.at[n]) for n, (src, dst) in enumerate(pairs)]
    for c in copies:
        c.start()
    for c in copies:
        c.wait()


def body(q_raw, k_raw, values, grad_out, gain_q, gain_k, pair_blocks, pair_count):
    def vmem(*shape, dtype=jnp.float32):
        return pltpu.VMEM(shape, dtype)

    low = jnp.bfloat16
    tile = (HEADS, ROWS, HEAD_DIM)
    square = (BITS + 1, HEADS, ROWS, ROWS)
    wide = jax.ShapeDtypeStruct((ROWS, HEADS * HEAD_DIM), low)
    narrow = jax.ShapeDtypeStruct((1, HEAD_DIM), jnp.float32)
    any_space = pl.BlockSpec(memory_space=pl.ANY)
    in_vmem = pl.BlockSpec(memory_space=pltpu.VMEM)
    in_smem = pl.BlockSpec(memory_space=pltpu.SMEM)
    pair = pltpu.SemaphoreType.DMA((BITS, HEADS))
    parts = pl.pallas_call(
        kernel,
        out_shape=(wide, wide, wide, jax.ShapeDtypeStruct((2, HEAD_DIM), jnp.float32)),
        in_specs=[any_space] * 4 + [in_vmem] * 2 + [in_smem] * 2,
        out_specs=(any_space, any_space, any_space, in_vmem),
        scratch_shapes=[
            vmem(*tile, dtype=low), vmem(*tile, dtype=low),
            vmem(*tile, dtype=low), vmem(*tile, dtype=low), vmem(*tile, dtype=low), vmem(*tile, dtype=low),
            vmem(BITS, *tile, dtype=low), vmem(BITS, *tile, dtype=low),
            vmem(*tile), vmem(*tile), vmem(*tile), vmem(*tile),
            vmem(*square), vmem(*square),
            vmem(HEADS, 2, ROWS), vmem(BITS, HEADS, 2, ROWS), vmem(BITS, HEADS, 2, ROWS),
            vmem(HEADS, 2, ROWS), vmem(BITS, HEADS, 2, ROWS), vmem(BITS, HEADS, 2, ROWS),
            vmem(*tile), vmem(*tile), vmem(*tile), vmem(BITS, *tile, dtype=low), vmem(BITS, *tile, dtype=low),
            vmem(*tile, dtype=low), vmem(*tile, dtype=low), vmem(*tile, dtype=low),
            vmem(3, 8, HEAD_DIM),
            vmem(HEAD_DEVS, 2, HEAD_DIM), vmem(Y_DEVS, 2, HEAD_DIM), vmem(Z_DEVS, 2, HEAD_DIM),
            pltpu.SemaphoreType.DMA((4, HEADS)), pltpu.SemaphoreType.DMA((3, HEADS)),
            pair, pair, pair, pair, pair, pair, pair, pair, pair, pair,
            pltpu.SemaphoreType.DMA((PEERS,)), pltpu.SemaphoreType.DMA((PEERS,)),
        ],
        compiler_params=pltpu.CompilerParams(
            collective_id=0, has_side_effects=True, vmem_limit_bytes=63 * 1024 * 1024
        ),
        cost_estimate=pl.CostEstimate(
            flops=2 * 5 * 15 * ROWS * ROWS * HEAD_DIM,
            bytes_accessed=7 * ROWS * HEADS * HEAD_DIM * 2,
            transcendentals=15 * ROWS * ROWS,
        ),
    )(
        q_raw, k_raw, values, grad_out,
        gain_q.reshape(1, HEAD_DIM), gain_k.reshape(1, HEAD_DIM), pair_blocks, pair_count,
    )
    grad_q, grad_k, grad_v, sum_q, sum_k = pl.pallas_call(
        hand_over,
        out_shape=(wide, wide, wide, narrow, narrow),
        in_specs=[in_vmem] * 4,
        out_specs=(any_space,) * 5,
        scratch_shapes=[pltpu.SemaphoreType.DMA((5,))],
        compiler_params=pltpu.CompilerParams(has_side_effects=True, vmem_limit_bytes=63 * 1024 * 1024),
    )(*parts)
    return grad_q, grad_k, grad_v, sum_q.reshape(HEAD_DIM), sum_k.reshape(HEAD_DIM)


def solution(mesh):
    placed = (
        P("ctx", "head"),
        P("ctx", "head"),
        P("ctx", "head"),
        P("ctx", "head"),
        P(),
        P(),
        P("ctx", None),
        P("ctx"),
    )
    return jax.shard_map(
        body,
        mesh=mesh,
        in_specs=placed,
        out_specs=(P("ctx", "head"), P("ctx", "head"), P("ctx", "head"), P(), P()),
        check_vma=False,
    )
```

```python
import math

import jax
import jax.numpy as jnp
from jax import lax
from jax.experimental import pallas as pl
from jax.experimental.pallas import tpu as pltpu
from jax.sharding import PartitionSpec as P

HEAD_DIM = 128
BITS = 2
ROWS = 256
HEADS = 5
FLOOR_LOG = -1e30
FACTOR = 1.0 / math.sqrt(HEAD_DIM)
LOG2E = 1.0 / math.log(2.0)
HEAD_DEVS = 8
Y_DEVS = 4
Z_DEVS = 8
PIECES = 1
PEERS = (HEAD_DEVS - 1) + (Y_DEVS - 1) + (Z_DEVS - 1)
MESH = pl.DeviceIdType.MESH
ORDER = (
    "N0 Q0 N1 Q1",
    "N2 N3 N4 K0",
    "K1 K2 K3 K4",
    "L0 L1 L2 L3",
    "L4 F0 Q2 F1",
    "C0 Q3 G0 F2",
    "C1 Q4 G1 F3",
    "C2 G2 B0 D0",
    "H0 F4 C3 G3",
    "B1 D1 H1 C4",
    "G4 B2 D2 B3",
    "B4 A0 D3 H2",
    "H3 H4 E0 A1",
    "D4 E1 W0 W1",
    "A2 E2 W2 E3",
    "W3 E4 W4 A3",
)
NT = (((1,), (1,)), ((), ()))
NN = (((1,), (0,)), ((), ()))
TN = (((0,), (0,)), ((), ()))


def mm(a, b, dims):
    return lax.dot_general(a, b, dims, preferred_element_type=jnp.float32)


def kernel(
    q_hbm, k_hbm, v_hbm, g_hbm, gain_q_ref, gain_k_ref, blocks_ref, count_ref,
    oq_hbm, ok_hbm, ov_hbm, ogain_ref,
    raw_q, raw_k, qn, kn, vn, gn, rq, rg,
    q_hat, q_inv, k_hat, k_inv, prob, dprob, stat_own, stat_out, stat_in,
    fin_own, fin_out, fin_in, dq_own, dk_sum, dv_sum, dq_out, dq_in, oq, ok, ov, acc,
    sum_a, sum_b, sum_c,
    load_sem, store_sem, qs, qr, gs, gr, ss, sr, fs, fr, ds, dr, as_, ar,
):
    place = lax.axis_index("ctx")
    column = lax.axis_index("head")
    z = lax.rem(place, Z_DEVS)
    y = lax.div(place, Z_DEVS)
    partners = [jnp.bitwise_xor(place, 1 << i) for i in range(BITS)]
    lower = [jnp.bitwise_and(place, 1 << i) == 0 for i in range(BITS)]

    head_peers = [{"head": lax.rem(column + r, HEAD_DEVS)} for r in range(1, HEAD_DEVS)]
    y_peers = [{"ctx": lax.rem(y + r, Y_DEVS) * Z_DEVS + z} for r in range(1, Y_DEVS)]
    z_peers = [{"ctx": y * Z_DEVS + lax.rem(z + r, Z_DEVS)} for r in range(1, Z_DEVS)]

    barrier = pltpu.get_barrier_semaphore()
    for peer in z_peers + y_peers + head_peers:
        pl.semaphore_signal(barrier, 1, device_id=peer, device_id_type=MESH)

    def load(src, dst, slot, h):
        return pltpu.make_async_copy(
            src.at[:, h * HEAD_DIM : (h + 1) * HEAD_DIM], dst.at[h], load_sem.at[slot, h]
        )

    sources = ((g_hbm, gn), (q_hbm, raw_q), (k_hbm, raw_k), (v_hbm, vn))
    for slot, (src, dst) in enumerate(sources):
        for h in range(HEADS):
            load(src, dst, slot, h).start()

    def remote(src, dst, send, recv, peer):
        return pltpu.make_async_remote_copy(
            src_ref=src, dst_ref=dst, send_sem=send, recv_sem=recv,
            device_id=peer, device_id_type=MESH,
        )

    def q_copy(h, i):
        return remote(qn.at[h], rq.at[i, h], qs.at[i, h], qr.at[i, h], {"ctx": partners[i]})

    def g_copy(h, i):
        return remote(gn.at[h], rg.at[i, h], gs.at[i, h], gr.at[i, h], {"ctx": partners[i]})

    def s_copy(h, i):
        return remote(stat_out.at[i, h], stat_in.at[i, h], ss.at[i, h], sr.at[i, h], {"ctx": partners[i]})

    def f_copy(h, i):
        return remote(fin_out.at[i, h], fin_in.at[i, h], fs.at[i, h], fr.at[i, h], {"ctx": partners[i]})

    def d_copy(h, i):
        return remote(dq_out.at[i, h], dq_in.at[i, h], ds.at[i, h], dr.at[i, h], {"ctx": partners[i]})

    listed = []
    for i in range(BITS):
        hit = jnp.float32(0.0)
        for slot in range(BITS):
            live = (blocks_ref[0, slot] == partners[i]) & (slot < count_ref[0])
            hit = jnp.where(live, 1.0, hit)
        listed.append(hit)
    off = [jnp.where(lower[i], 1.0 - listed[i], 0.0) for i in range(BITS)]

    gain_q = gain_q_ref[...]
    gain_k = gain_k_ref[...]

    def norm(raw, gain, hat, inv, normed, h):
        x = raw[h].astype(jnp.float32)
        inverse = lax.rsqrt(jnp.mean(x * x, axis=1, keepdims=True) + 1e-06)
        x_hat = x * inverse
        hat[h] = x_hat
        inv[h] = jnp.broadcast_to(inverse, x.shape)
        normed[h] = (x_hat * gain).astype(jnp.bfloat16)

    def norm_query(h):
        load(q_hbm, raw_q, 1, h).wait()
        load(g_hbm, gn, 0, h).wait()
        norm(raw_q, gain_q, q_hat, q_inv, qn, h)

    def send(h):
        if h == 0:
            pl.semaphore_wait(barrier, PEERS)
        for i in (1, 0):
            g_copy(h, i).start()
            q_copy(h, i).start()

    def norm_key(h):
        load(k_hbm, raw_k, 2, h).wait()
        load(v_hbm, vn, 3, h).wait()
        norm(raw_k, gain_k, k_hat, k_inv, kn, h)

    acc[...] = jnp.zeros_like(acc)

    def forward(h, slot, query, grad):
        scores = mm(kn[h], query, NT)
        largest = jnp.max(scores, axis=0, keepdims=True)
        e = jnp.exp2((scores - largest) * (FACTOR * LOG2E))
        total = jnp.sum(e, axis=0, keepdims=True)
        p = e * (1.0 / total)
        dp = mm(vn[h], grad, NT)
        prob[slot, h] = p
        dprob[slot, h] = dp
        dot = jnp.sum(p.astype(jnp.bfloat16).astype(jnp.float32) * dp, axis=0, keepdims=True)
        return largest * FACTOR + jnp.log(total), dot

    def far_forward(h):
        for i in (0, 1):
            g_copy(h, i).wait_recv()
            q_copy(h, i).wait_recv()
            log, dot = forward(h, i + 1, rq[i, h], rg[i, h])
            stat_out[i, h, 0:1] = jnp.where(off[i] > 0.5, FLOOR_LOG, log)
            stat_out[i, h, 1:2] = dot
            s_copy(h, i).start()

    def near_forward(h):
        log, dot = forward(h, 0, qn[h], gn[h])
        stat_own[h, 0:1] = log
        stat_own[h, 1:2] = dot

    def combine(h):
        logs = [stat_own[h, 0:1]]
        dots = [stat_own[h, 1:2]]
        for i in range(BITS):
            s_copy(h, i).wait_recv()
            logs.append(jnp.where(off[i] > 0.5, FLOOR_LOG, stat_in[i, h, 0:1]))
            dots.append(stat_in[i, h, 1:2])
        top = jnp.maximum(jnp.maximum(logs[0], logs[1]), logs[2])
        parts = [jnp.exp(log - top) for log in logs]
        inverse = 1.0 / (parts[0] + parts[1] + parts[2])
        shares = [part * inverse for part in parts]
        row_dot = shares[0] * dots[0] + shares[1] * dots[1] + shares[2] * dots[2]
        for i in range(BITS):
            fin_out[i, h, 0:1] = shares[i + 1]
            fin_out[i, h, 1:2] = row_dot
            f_copy(h, i).start()
        fin_own[h, 0:1] = shares[0]
        fin_own[h, 1:2] = row_dot

    def one_back(h, slot, query, grad, share, row_dot):
        w = prob[slot, h] * share
        ds_t = (w * (dprob[slot, h] - row_dot) * FACTOR).astype(jnp.bfloat16)
        dv = mm(w.astype(jnp.bfloat16), grad, NN)
        dk = mm(ds_t, query, NN)
        dq = mm(ds_t, kn[h], TN)
        return dq, dk, dv

    def norm_back(hat, inv, gain, grad):
        gg = grad * gain
        inner = jnp.mean(hat * gg, axis=1, keepdims=True)
        return (inv * (gg - hat * inner)).astype(jnp.bfloat16)

    def fold(a):
        return jnp.sum(a.reshape(ROWS // 8, 8, HEAD_DIM), axis=0)

    def columns(h):
        return slice(h * HEAD_DIM, (h + 1) * HEAD_DIM)

    def store(src, dst, slot, h):
        return pltpu.make_async_copy(src.at[h], dst.at[:, columns(h)], store_sem.at[slot, h])

    def near_back(h):
        dq, dk, dv = one_back(h, 0, qn[h], gn[h], fin_own[h, 0:1], fin_own[h, 1:2])
        dq_own[h] = dq
        dk_sum[h] = dk
        dv_sum[h] = dv
        acc[0] += fold(dq * q_hat[h])

    def far_back(h):
        gk, gv = dk_sum[h], dv_sum[h]
        for i in (1, 0):
            f_copy(h, i).wait_recv()
            dq, dk, dv = one_back(
                h, i + 1, rq[i, h], rg[i, h], fin_in[i, h, 0:1], fin_in[i, h, 1:2]
            )
            dq_out[i, h] = dq.astype(jnp.bfloat16)
            acc[1] += fold(dq * rq[i, h].astype(jnp.float32))
            gk, gv = gk + dk, gv + dv
        dk_sum[h] = gk
        dv_sum[h] = gv
        acc[2] += fold(gk * k_hat[h])

    def write_kv(h):
        ov[h] = dv_sum[h].astype(jnp.bfloat16)
        store(ov, ov_hbm, 2, h).start()
        ok[h] = norm_back(k_hat[h], k_inv[h], gain_k, dk_sum[h])
        store(ok, ok_hbm, 1, h).start()

    def send_dq(h):
        for i in (1, 0):
            d_copy(h, i).start()

    def finish(h):
        for i in range(BITS):
            d_copy(h, i).wait_recv()
        gq = dq_own[h] + dq_in[0, h].astype(jnp.float32) + dq_in[1, h].astype(jnp.float32)
        oq[h] = norm_back(q_hat[h], q_inv[h], gain_q, gq)
        store(oq, oq_hbm, 0, h).start()

    def share_copies(buffer, index, peers, base):
        return [
            remote(buffer.at[index], buffer.at[index], as_.at[base + r], ar.at[base + r], peer)
            for r, peer in enumerate(peers)
        ]

    copies_a = share_copies(sum_a, column, head_peers, 0)
    copies_b = share_copies(sum_b, y, y_peers, HEAD_DEVS - 1)
    copies_c = share_copies(sum_c, z, z_peers, HEAD_DEVS + Y_DEVS - 2)

    def gain_sums(stage):
        if stage == 0:
            part_q = jnp.sum(acc[0], axis=0, keepdims=True)
            part_q += jnp.sum(acc[1], axis=0, keepdims=True) / gain_q
            sum_a[column, 0:1] = part_q
            sum_a[column, 1:2] = jnp.sum(acc[2], axis=0, keepdims=True)
            for c in copies_a:
                c.start()
        elif stage == 1:
            for c in copies_a:
                c.wait_recv()
            sum_b[y] = jnp.sum(sum_a[...], axis=0)
            for c in copies_b:
                c.start()
        elif stage == 2:
            for c in copies_a:
                c.wait_send()
            for c in copies_b:
                c.wait_recv()
            sum_c[z] = jnp.sum(sum_b[...], axis=0)
            for c in copies_c:
                c.start()
        else:
            for c in copies_b:
                c.wait_send()
            for c in copies_c:
                c.wait_recv()
            total = jnp.sum(sum_c[...], axis=0)
            ogain_ref[...] = total

    def wait_sent(h):
        for i in range(BITS):
            for copy in (q_copy, g_copy, s_copy, f_copy, d_copy):
                copy(h, i).wait_send()
        for slot, (src, dst) in enumerate(((oq, oq_hbm), (ok, ok_hbm), (ov, ov_hbm))):
            store(src, dst, slot, h).wait()

    steps = {
        "N": norm_query, "Q": send, "K": norm_key, "L": near_forward, "F": far_forward,
        "C": combine, "G": near_back, "B": far_back, "H": write_kv, "W": wait_sent, "D": send_dq, "E": finish, "A": gain_sums,
    }
    for line in ORDER:
        for word in line.split():
            steps[word[0]](int(word[1]))

    for c in copies_c:
        c.wait_send()


def hand_over(q, k, v, gains, oq, ok, ov, ogain_q, ogain_k, sem):
    pairs = ((q, oq), (k, ok), (v, ov), (gains.at[0:1], ogain_q), (gains.at[1:2], ogain_k))
    copies = [pltpu.make_async_copy(src, dst, sem.at[n]) for n, (src, dst) in enumerate(pairs)]
    for c in copies:
        c.start()
    for c in copies:
        c.wait()


def body(q_raw, k_raw, values, grad_out, gain_q, gain_k, pair_blocks, pair_count):
    def vmem(*shape, dtype=jnp.float32):
        return pltpu.VMEM(shape, dtype)

    low = jnp.bfloat16
    tile = (HEADS, ROWS, HEAD_DIM)
    square = (BITS + 1, HEADS, ROWS, ROWS)
    wide = jax.ShapeDtypeStruct((ROWS, HEADS * HEAD_DIM), low)
    narrow = jax.ShapeDtypeStruct((1, HEAD_DIM), jnp.float32)
    any_space = pl.BlockSpec(memory_space=pl.ANY)
    in_vmem = pl.BlockSpec(memory_space=pltpu.VMEM)
    in_smem = pl.BlockSpec(memory_space=pltpu.SMEM)
    pair = pltpu.SemaphoreType.DMA((BITS, HEADS))
    parts = pl.pallas_call(
        kernel,
        out_shape=(pltpu.VMEM((ROWS, HEADS * HEAD_DIM), low),) * 3 + (pltpu.VMEM((2, HEAD_DIM), jnp.float32),),
        in_specs=[any_space] * 4 + [in_vmem] * 2 + [in_smem] * 2,
        out_specs=(any_space, any_space, any_space, in_vmem),
        scratch_shapes=[
            vmem(*tile, dtype=low), vmem(*tile, dtype=low),
            vmem(*tile, dtype=low), vmem(*tile, dtype=low), vmem(*tile, dtype=low), vmem(*tile, dtype=low),
            vmem(BITS, *tile, dtype=low), vmem(BITS, *tile, dtype=low),
            vmem(*tile), vmem(*tile), vmem(*tile), vmem(*tile),
            vmem(*square), vmem(*square),
            vmem(HEADS, 2, ROWS), vmem(BITS, HEADS, 2, ROWS), vmem(BITS, HEADS, 2, ROWS),
            vmem(HEADS, 2, ROWS), vmem(BITS, HEADS, 2, ROWS), vmem(BITS, HEADS, 2, ROWS),
            vmem(*tile), vmem(*tile), vmem(*tile), vmem(BITS, *tile, dtype=low), vmem(BITS, *tile, dtype=low),
            vmem(*tile, dtype=low), vmem(*tile, dtype=low), vmem(*tile, dtype=low),
            vmem(3, 8, HEAD_DIM),
            vmem(HEAD_DEVS, 2, HEAD_DIM), vmem(Y_DEVS, 2, HEAD_DIM), vmem(Z_DEVS, 2, HEAD_DIM),
            pltpu.SemaphoreType.DMA((4, HEADS)), pltpu.SemaphoreType.DMA((3, HEADS)),
            pair, pair, pair, pair, pair, pair, pair, pair, pair, pair,
            pltpu.SemaphoreType.DMA((PEERS,)), pltpu.SemaphoreType.DMA((PEERS,)),
        ],
        compiler_params=pltpu.CompilerParams(
            collective_id=0, has_side_effects=True, vmem_limit_bytes=56 * 1024 * 1024
        ),
        cost_estimate=pl.CostEstimate(
            flops=2 * 5 * 15 * ROWS * ROWS * HEAD_DIM,
            bytes_accessed=7 * ROWS * HEADS * HEAD_DIM * 2,
            transcendentals=15 * ROWS * ROWS,
        ),
    )(
        *[
            pltpu.with_memory_space_constraint(x, pltpu.HBM)
            for x in (q_raw, k_raw, values, grad_out, gain_q.reshape(1, HEAD_DIM), gain_k.reshape(1, HEAD_DIM))
        ],
        pair_blocks, pair_count,
    )
    grad_q, grad_k, grad_v, sum_q, sum_k = pl.pallas_call(
        hand_over,
        out_shape=(wide, wide, wide, narrow, narrow),
        in_specs=[any_space] * 4,
        out_specs=(any_space,) * 5,
        scratch_shapes=[pltpu.SemaphoreType.DMA((5,))],
        compiler_params=pltpu.CompilerParams(has_side_effects=True, vmem_limit_bytes=16 * 1024 * 1024),
    )(*parts)
    return grad_q, grad_k, grad_v, sum_q.reshape(HEAD_DIM), sum_k.reshape(HEAD_DIM)


def solution(mesh):
    placed = (
        P("ctx", "head"),
        P("ctx", "head"),
        P("ctx", "head"),
        P("ctx", "head"),
        P(),
        P(),
        P("ctx", None),
        P("ctx"),
    )
    return jax.shard_map(
        body,
        mesh=mesh,
        in_specs=placed,
        out_specs=(P("ctx", "head"), P("ctx", "head"), P("ctx", "head"), P(), P()),
        check_vma=False,
    )
```

```python
import math

import jax
import jax.numpy as jnp
from jax import lax
from jax.experimental import pallas as pl
from jax.experimental.pallas import tpu as pltpu
from jax.sharding import PartitionSpec as P

HEAD_DIM = 128
BITS = 2
ROWS = 256
HEADS = 5
FLOOR_LOG = -1e30
FACTOR = 1.0 / math.sqrt(HEAD_DIM)
LOG2E = 1.0 / math.log(2.0)
HEAD_DEVS = 8
Y_DEVS = 4
Z_DEVS = 8
PEERS = (HEAD_DEVS - 1) + (Y_DEVS - 1) + (Z_DEVS - 1)
MESH = pl.DeviceIdType.MESH
ORDER = (
    "N0 Q0 J0 J1",
    "J2 J3 J4 N1",
    "Q1 N2 N3 N4",
    "K0 K1 K2 K3",
    "K4 L0 L1 L2",
    "L3 L4 M0 F0",
    "Q2 F1 C0 Q3",
    "G0 F2 V0 B0",
    "C1 Q4 G1 B1",
    "F3 C2 G2 B2",
    "F4 D0 D1 H0",
    "C3 G3 B3 C4",
    "G4 B4 A0 D2",
    "H1 H2 H3 H4",
    "E0 A1 D3 E1",
    "W0 W1 A2 D4",
    "E2 W2 E3 W3",
    "E4 W4 A3",
)
NT = (((1,), (1,)), ((), ()))
NN = (((1,), (0,)), ((), ()))
TN = (((0,), (0,)), ((), ()))


def mm(a, b, dims):
    return lax.dot_general(a, b, dims, preferred_element_type=jnp.float32)


def kernel(
    q_hbm, k_hbm, v_hbm, g_hbm, gain_q_ref, gain_k_ref, blocks_ref, count_ref,
    oq_hbm, ok_hbm, ov_hbm, ogain_ref,
    raw_q, raw_k, qn, kn, vn, gn, rq, rg,
    q_hat, q_inv, k_hat, k_inv, prob, dprob, near_out, near_in,
    stat_out, stat_in, cross_in, fin_own, dq_own, dk_sum, dv_sum, dq_out, dq_in, oq, ok, ov, acc,
    sum_a, sum_b, sum_c,
    load_sem, store_sem, qs, qr, gs, gr, ss, sr, ns, nr, xs, xr, ds, dr, as_, ar,
):
    place = lax.axis_index("ctx")
    column = lax.axis_index("head")
    z = lax.rem(place, Z_DEVS)
    y = lax.div(place, Z_DEVS)
    partners = [jnp.bitwise_xor(place, 1 << i) for i in range(BITS)]
    across = {"ctx": jnp.bitwise_xor(place, 3)}
    lower = [jnp.bitwise_and(place, 1 << i) == 0 for i in range(BITS)]

    head_peers = [{"head": lax.rem(column + r, HEAD_DEVS)} for r in (4, 5, 3, 2, 6, 1, 7)]
    y_peers = [{"ctx": lax.rem(y + r, Y_DEVS) * Z_DEVS + z} for r in (2, 1, 3)]
    z_peers = [{"ctx": y * Z_DEVS + lax.rem(z + r, Z_DEVS)} for r in (4, 3, 5, 2, 6, 1, 7)]

    barrier = pltpu.get_barrier_semaphore()
    for peer in z_peers + y_peers + head_peers:
        pl.semaphore_signal(barrier, 1, device_id=peer, device_id_type=MESH)

    def load(src, dst, slot, h):
        return pltpu.make_async_copy(
            src.at[:, h * HEAD_DIM : (h + 1) * HEAD_DIM], dst.at[h], load_sem.at[slot, h]
        )

    for h in range(HEADS):
        load(g_hbm, gn, 0, h).start()
        load(q_hbm, raw_q, 1, h).start()

    def remote(src, dst, send, recv, peer):
        return pltpu.make_async_remote_copy(
            src_ref=src, dst_ref=dst, send_sem=send, recv_sem=recv,
            device_id=peer, device_id_type=MESH,
        )

    def q_copy(h, i):
        return remote(qn.at[h], rq.at[i, h], qs.at[i, h], qr.at[i, h], {"ctx": partners[i]})

    def g_copy(h, i):
        return remote(gn.at[h], rg.at[i, h], gs.at[i, h], gr.at[i, h], {"ctx": partners[i]})

    def s_copy(h, i):
        return remote(stat_out.at[h, i], stat_in.at[h, i], ss.at[i, h], sr.at[i, h], {"ctx": partners[i]})

    def x_copy(h):
        return remote(stat_out.at[h], cross_in.at[h], xs.at[h], xr.at[h], across)

    def n_copy(i):
        return remote(near_out, near_in.at[i], ns.at[i], nr.at[i], {"ctx": partners[i]})

    def d_copy(h, i):
        return remote(dq_out.at[i, h], dq_in.at[i, h], ds.at[i, h], dr.at[i, h], {"ctx": partners[i]})

    listed = []
    for i in range(BITS):
        hit = jnp.float32(0.0)
        for slot in range(BITS):
            live = (blocks_ref[0, slot] == partners[i]) & (slot < count_ref[0])
            hit = jnp.where(live, 1.0, hit)
        listed.append(hit)
    off = [jnp.where(lower[i], 1.0 - listed[i], 0.0) for i in range(BITS)]

    gain_q = gain_q_ref[...]
    gain_k = gain_k_ref[...]

    def norm(raw, gain, hat, inv, normed, h):
        x = raw[h].astype(jnp.float32)
        inverse = lax.rsqrt(jnp.mean(x * x, axis=1, keepdims=True) + 1e-06)
        x_hat = x * inverse
        hat[h] = x_hat
        inv[h] = jnp.broadcast_to(inverse, x.shape)
        normed[h] = (x_hat * gain).astype(jnp.bfloat16)

    def norm_query(h):
        load(q_hbm, raw_q, 1, h).wait()
        load(g_hbm, gn, 0, h).wait()
        norm(raw_q, gain_q, q_hat, q_inv, qn, h)

    def send(h):
        if h == 0:
            pl.semaphore_wait(barrier, PEERS)
        for i in (1, 0):
            g_copy(h, i).start()
            q_copy(h, i).start()

    def load_kv(h):
        load(k_hbm, raw_k, 2, h).start()
        load(v_hbm, vn, 3, h).start()

    def norm_key(h):
        load(k_hbm, raw_k, 2, h).wait()
        load(v_hbm, vn, 3, h).wait()
        norm(raw_k, gain_k, k_hat, k_inv, kn, h)

    acc[...] = jnp.zeros_like(acc)

    def forward(h, slot, query, grad):
        scores = mm(kn[h], query, NT)
        largest = jnp.max(scores, axis=0, keepdims=True)
        e = jnp.exp2((scores - largest) * (FACTOR * LOG2E))
        total = jnp.sum(e, axis=0, keepdims=True)
        p = e * (1.0 / total)
        dp = mm(vn[h], grad, NT)
        prob[slot, h] = p
        dprob[slot, h] = dp
        dot = jnp.sum(p.astype(jnp.bfloat16).astype(jnp.float32) * dp, axis=0, keepdims=True)
        return largest * FACTOR + jnp.log(total), dot

    def far_forward(h):
        for i in (0, 1):
            g_copy(h, i).wait_recv()
            q_copy(h, i).wait_recv()
            log, dot = forward(h, i + 1, rq[i, h], rg[i, h])
            stat_out[h, i, 0:1] = jnp.where(off[i] > 0.5, FLOOR_LOG, log)
            stat_out[h, i, 1:2] = dot
            if i == 1:
                x_copy(h).start()
            s_copy(h, i).start()

    def near_forward(h):
        log, dot = forward(h, 0, qn[h], gn[h])
        near_out[h, 0:1] = log
        near_out[h, 1:2] = dot
        for i in range(BITS):
            near_out[h, 2 + i : 3 + i] = jnp.full((1, ROWS), off[i], jnp.float32)

    def send_near(h):
        for i in (1, 0):
            n_copy(i).start()

    def wait_near(h):
        for i in range(BITS):
            n_copy(i).wait_recv()

    def shares_of(logs, dots):
        top = jnp.maximum(jnp.maximum(logs[0], logs[1]), logs[2])
        parts = [jnp.exp(log - top) for log in logs]
        inverse = 1.0 / (parts[0] + parts[1] + parts[2])
        row_dot = (parts[0] * dots[0] + parts[1] * dots[1] + parts[2] * dots[2]) * inverse
        return parts[0] * inverse, row_dot

    def combine(h):
        logs = [near_out[h, 0:1]]
        dots = [near_out[h, 1:2]]
        for i in range(BITS):
            s_copy(h, i).wait_recv()
            logs.append(jnp.where(off[i] > 0.5, FLOOR_LOG, stat_in[h, i, 0:1]))
            dots.append(stat_in[h, i, 1:2])
        fin_own[h, 0:1], fin_own[h, 1:2] = shares_of(logs, dots)

    def far_shares(h, i):
        other = 1 - i
        logs = [
            jnp.where(near_in[i, h, 2 + i : 3 + i] > 0.5, FLOOR_LOG, stat_out[h, i, 0:1]),
            near_in[i, h, 0:1],
            jnp.where(near_in[i, h, 2 + other : 3 + other] > 0.5, FLOOR_LOG, cross_in[h, other, 0:1]),
        ]
        dots = [stat_out[h, i, 1:2], near_in[i, h, 1:2], cross_in[h, other, 1:2]]
        return shares_of(logs, dots)

    def one_back(h, slot, query, grad, share, row_dot):
        w = prob[slot, h] * share
        ds_t = (w * (dprob[slot, h] - row_dot) * FACTOR).astype(jnp.bfloat16)
        dv = mm(w.astype(jnp.bfloat16), grad, NN)
        dk = mm(ds_t, query, NN)
        dq = mm(ds_t, kn[h], TN)
        return dq, dk, dv

    def norm_back(hat, inv, gain, grad):
        gg = grad * gain
        inner = jnp.mean(hat * gg, axis=1, keepdims=True)
        return (inv * (gg - hat * inner)).astype(jnp.bfloat16)

    def fold(a):
        return jnp.sum(a.reshape(ROWS // 8, 8, HEAD_DIM), axis=0)

    def columns(h):
        return slice(h * HEAD_DIM, (h + 1) * HEAD_DIM)

    def store(src, dst, slot, h):
        return pltpu.make_async_copy(src.at[h], dst.at[:, columns(h)], store_sem.at[slot, h])

    def near_back(h):
        dq, dk, dv = one_back(h, 0, qn[h], gn[h], fin_own[h, 0:1], fin_own[h, 1:2])
        dq_own[h] = dq
        dk_sum[h] = dk
        dv_sum[h] = dv
        acc[0] += fold(dq * q_hat[h])

    def far_back(h):
        gk, gv = dk_sum[h], dv_sum[h]
        x_copy(h).wait_recv()
        for i in (1, 0):
            share, row_dot = far_shares(h, i)
            dq, dk, dv = one_back(h, i + 1, rq[i, h], rg[i, h], share, row_dot)
            dq_out[i, h] = dq.astype(jnp.bfloat16)
            acc[1] += fold(dq * rq[i, h].astype(jnp.float32))
            gk, gv = gk + dk, gv + dv
        dk_sum[h] = gk
        dv_sum[h] = gv
        acc[2] += fold(gk * k_hat[h])

    def write_kv(h):
        ov[h] = dv_sum[h].astype(jnp.bfloat16)
        store(ov, ov_hbm, 2, h).start()
        ok[h] = norm_back(k_hat[h], k_inv[h], gain_k, dk_sum[h])
        store(ok, ok_hbm, 1, h).start()

    def send_dq(h):
        for i in (1, 0):
            d_copy(h, i).start()

    def finish(h):
        for i in range(BITS):
            d_copy(h, i).wait_recv()
        gq = dq_own[h] + dq_in[0, h].astype(jnp.float32) + dq_in[1, h].astype(jnp.float32)
        oq[h] = norm_back(q_hat[h], q_inv[h], gain_q, gq)
        store(oq, oq_hbm, 0, h).start()

    def share_copies(buffer, index, peers, base):
        return [
            remote(buffer.at[index], buffer.at[index], as_.at[base + r], ar.at[base + r], peer)
            for r, peer in enumerate(peers)
        ]

    copies_a = share_copies(sum_a, column, head_peers, 0)
    copies_b = share_copies(sum_b, y, y_peers, HEAD_DEVS - 1)
    copies_c = share_copies(sum_c, z, z_peers, HEAD_DEVS + Y_DEVS - 2)

    def gain_sums(stage):
        if stage == 0:
            part_q = jnp.sum(acc[0], axis=0, keepdims=True)
            part_q += jnp.sum(acc[1], axis=0, keepdims=True) / gain_q
            sum_a[column, 0:1] = part_q
            sum_a[column, 1:2] = jnp.sum(acc[2], axis=0, keepdims=True)
            for c in copies_a:
                c.start()
        elif stage == 1:
            for c in copies_a:
                c.wait_recv()
            sum_b[y] = jnp.sum(sum_a[...], axis=0)
            for c in copies_b:
                c.start()
        elif stage == 2:
            for c in copies_a:
                c.wait_send()
            for c in copies_b:
                c.wait_recv()
            sum_c[z] = jnp.sum(sum_b[...], axis=0)
            for c in copies_c:
                c.start()
        else:
            for c in copies_b:
                c.wait_send()
            for c in copies_c:
                c.wait_recv()
            total = jnp.sum(sum_c[...], axis=0)
            ogain_ref[...] = total

    def wait_sent(h):
        for i in range(BITS):
            for copy in (q_copy, g_copy, s_copy, d_copy):
                copy(h, i).wait_send()
        x_copy(h).wait_send()
        if h == 0:
            for i in range(BITS):
                n_copy(i).wait_send()
        for slot, (src, dst) in enumerate(((oq, oq_hbm), (ok, ok_hbm), (ov, ov_hbm))):
            store(src, dst, slot, h).wait()

    steps = {
        "N": norm_query, "Q": send, "K": norm_key, "L": near_forward, "F": far_forward,
        "C": combine, "J": load_kv, "M": send_near, "V": wait_near, "G": near_back, "B": far_back, "H": write_kv, "W": wait_sent, "D": send_dq, "E": finish, "A": gain_sums,
    }
    for line in ORDER:
        for word in line.split():
            steps[word[0]](int(word[1]))

    for c in copies_c:
        c.wait_send()


def hand_over(q, k, v, gains, oq, ok, ov, ogain_q, ogain_k, sem):
    pairs = ((q, oq), (k, ok), (v, ov), (gains.at[0:1], ogain_q), (gains.at[1:2], ogain_k))
    copies = [pltpu.make_async_copy(src, dst, sem.at[n]) for n, (src, dst) in enumerate(pairs)]
    for c in copies:
        c.start()
    for c in copies:
        c.wait()


def body(q_raw, k_raw, values, grad_out, gain_q, gain_k, pair_blocks, pair_count):
    def vmem(*shape, dtype=jnp.float32):
        return pltpu.VMEM(shape, dtype)

    low = jnp.bfloat16
    tile = (HEADS, ROWS, HEAD_DIM)
    square = (BITS + 1, HEADS, ROWS, ROWS)
    wide = jax.ShapeDtypeStruct((ROWS, HEADS * HEAD_DIM), low)
    narrow = jax.ShapeDtypeStruct((1, HEAD_DIM), jnp.float32)
    any_space = pl.BlockSpec(memory_space=pl.ANY)
    in_vmem = pl.BlockSpec(memory_space=pltpu.VMEM)
    in_smem = pl.BlockSpec(memory_space=pltpu.SMEM)
    pair = pltpu.SemaphoreType.DMA((BITS, HEADS))
    parts = pl.pallas_call(
        kernel,
        out_shape=(pltpu.VMEM((ROWS, HEADS * HEAD_DIM), low),) * 3 + (pltpu.VMEM((2, HEAD_DIM), jnp.float32),),
        in_specs=[any_space] * 4 + [in_vmem] * 2 + [in_smem] * 2,
        out_specs=(any_space, any_space, any_space, in_vmem),
        scratch_shapes=[
            vmem(*tile, dtype=low), vmem(*tile, dtype=low),
            vmem(*tile, dtype=low), vmem(*tile, dtype=low), vmem(*tile, dtype=low), vmem(*tile, dtype=low),
            vmem(BITS, *tile, dtype=low), vmem(BITS, *tile, dtype=low),
            vmem(*tile), vmem(*tile), vmem(*tile), vmem(*tile),
            vmem(*square), vmem(*square),
            vmem(HEADS, 4, ROWS), vmem(BITS, HEADS, 4, ROWS),
            vmem(HEADS, BITS, 2, ROWS), vmem(HEADS, BITS, 2, ROWS), vmem(HEADS, BITS, 2, ROWS),
            vmem(HEADS, 2, ROWS),
            vmem(*tile), vmem(*tile), vmem(*tile), vmem(BITS, *tile, dtype=low), vmem(BITS, *tile, dtype=low),
            vmem(*tile, dtype=low), vmem(*tile, dtype=low), vmem(*tile, dtype=low),
            vmem(3, 8, HEAD_DIM),
            vmem(HEAD_DEVS, 2, HEAD_DIM), vmem(Y_DEVS, 2, HEAD_DIM), vmem(Z_DEVS, 2, HEAD_DIM),
            pltpu.SemaphoreType.DMA((4, HEADS)), pltpu.SemaphoreType.DMA((3, HEADS)),
            pair, pair, pair, pair, pair, pair,
            pltpu.SemaphoreType.DMA((BITS,)), pltpu.SemaphoreType.DMA((BITS,)),
            pltpu.SemaphoreType.DMA((HEADS,)), pltpu.SemaphoreType.DMA((HEADS,)), pair, pair,
            pltpu.SemaphoreType.DMA((PEERS,)), pltpu.SemaphoreType.DMA((PEERS,)),
        ],
        compiler_params=pltpu.CompilerParams(
            collective_id=0, has_side_effects=True, vmem_limit_bytes=56 * 1024 * 1024
        ),
        cost_estimate=pl.CostEstimate(
            flops=2 * 5 * 15 * ROWS * ROWS * HEAD_DIM,
            bytes_accessed=7 * ROWS * HEADS * HEAD_DIM * 2,
            transcendentals=15 * ROWS * ROWS,
        ),
    )(
        *[
            pltpu.with_memory_space_constraint(x, pltpu.HBM)
            for x in (q_raw, k_raw, values, grad_out, gain_q.reshape(1, HEAD_DIM), gain_k.reshape(1, HEAD_DIM))
        ],
        pair_blocks, pair_count,
    )
    grad_q, grad_k, grad_v, sum_q, sum_k = pl.pallas_call(
        hand_over,
        out_shape=(wide, wide, wide, narrow, narrow),
        in_specs=[any_space] * 4,
        out_specs=(any_space,) * 5,
        scratch_shapes=[pltpu.SemaphoreType.DMA((5,))],
        compiler_params=pltpu.CompilerParams(has_side_effects=True, vmem_limit_bytes=16 * 1024 * 1024),
    )(*parts)
    return grad_q, grad_k, grad_v, sum_q.reshape(HEAD_DIM), sum_k.reshape(HEAD_DIM)


def solution(mesh):
    placed = (
        P("ctx", "head"),
        P("ctx", "head"),
        P("ctx", "head"),
        P("ctx", "head"),
        P(),
        P(),
        P("ctx", None),
        P("ctx"),
    )
    return jax.shard_map(
        body,
        mesh=mesh,
        in_specs=placed,
        out_specs=(P("ctx", "head"), P("ctx", "head"), P("ctx", "head"), P(), P()),
        check_vma=False,
    )
```

```python
import math

import jax
import jax.numpy as jnp
from jax import lax
from jax.experimental import pallas as pl
from jax.experimental.pallas import tpu as pltpu
from jax.sharding import PartitionSpec as P

HEAD_DIM = 128
BITS = 2
ROWS = 256
HEADS = 5
FLOOR_LOG = -1e30
FACTOR = 1.0 / math.sqrt(HEAD_DIM)
LOG2E = 1.0 / math.log(2.0)
HEAD_DEVS = 8
Y_DEVS = 4
Z_DEVS = 8
PEERS = (HEAD_DEVS - 1) + (Y_DEVS - 1) + (Z_DEVS - 1)
MESH = pl.DeviceIdType.MESH
ORDER = (
    "N0 Q0 J0 J1",
    "J2 J3 J4 N1",
    "Q1 N2 N3 N4",
    "K0 K1 K2 K3",
    "K4 L0 L1 L2",
    "L3 L4 M0 F0",
    "Q2 F1 C0 Q3",
    "G0 F2 V0 B0",
    "C1 Q4 G1 B1",
    "F3 C2 G2 B2",
    "F4 D0 C3 G3",
    "B3 D1 C4 G4",
    "B4 A0 D2 H0",
    "H1 E0 A1 D3",
    "H2 H3 E1 W0",
    "W1 A2 D4 H4",
    "E2 W2 E3 W3",
    "E4 W4 A3",
)
NT = (((1,), (1,)), ((), ()))
NN = (((1,), (0,)), ((), ()))
TN = (((0,), (0,)), ((), ()))


def mm(a, b, dims):
    return lax.dot_general(a, b, dims, preferred_element_type=jnp.float32)


def kernel(
    q_hbm, k_hbm, v_hbm, g_hbm, gain_q_ref, gain_k_ref, blocks_ref, count_ref,
    oq_hbm, ok_hbm, ov_hbm, ogain_ref,
    raw_q, raw_k, qn, kn, vn, gn, rq, rg,
    q_hat, q_inv, k_hat, k_inv, prob, dprob, near_out, near_in,
    stat_out, stat_in, cross_in, fin_own, fin_far, dq_own, dk_sum, dv_sum, dq_out, dq_in, oq, ok, ov, acc,
    sum_a, sum_b, sum_c,
    load_sem, store_sem, qs, qr, gs, gr, ss, sr, ns, nr, xs, xr, ds, dr, as_, ar,
):
    place = lax.axis_index("ctx")
    column = lax.axis_index("head")
    z = lax.rem(place, Z_DEVS)
    y = lax.div(place, Z_DEVS)
    partners = [jnp.bitwise_xor(place, 1 << i) for i in range(BITS)]
    across = {"ctx": jnp.bitwise_xor(place, 3)}
    lower = [jnp.bitwise_and(place, 1 << i) == 0 for i in range(BITS)]

    head_peers = [{"head": lax.rem(column + r, HEAD_DEVS)} for r in (4, 5, 3, 2, 6, 1, 7)]
    y_peers = [{"ctx": lax.rem(y + r, Y_DEVS) * Z_DEVS + z} for r in (2, 1, 3)]
    z_peers = [{"ctx": y * Z_DEVS + lax.rem(z + r, Z_DEVS)} for r in (4, 3, 5, 2, 6, 1, 7)]

    barrier = pltpu.get_barrier_semaphore()
    for peer in z_peers + y_peers + head_peers:
        pl.semaphore_signal(barrier, 1, device_id=peer, device_id_type=MESH)

    def load(src, dst, slot, h):
        return pltpu.make_async_copy(
            src.at[:, h * HEAD_DIM : (h + 1) * HEAD_DIM], dst.at[h], load_sem.at[slot, h]
        )

    for h in range(HEADS):
        load(g_hbm, gn, 0, h).start()
        load(q_hbm, raw_q, 1, h).start()

    def remote(src, dst, send, recv, peer):
        return pltpu.make_async_remote_copy(
            src_ref=src, dst_ref=dst, send_sem=send, recv_sem=recv,
            device_id=peer, device_id_type=MESH,
        )

    def q_copy(h, i):
        return remote(qn.at[h], rq.at[i, h], qs.at[i, h], qr.at[i, h], {"ctx": partners[i]})

    def g_copy(h, i):
        return remote(gn.at[h], rg.at[i, h], gs.at[i, h], gr.at[i, h], {"ctx": partners[i]})

    def s_copy(h, i):
        return remote(stat_out.at[h, i], stat_in.at[h, i], ss.at[i, h], sr.at[i, h], {"ctx": partners[i]})

    def x_copy(h):
        return remote(stat_out.at[h], cross_in.at[h], xs.at[h], xr.at[h], across)

    def n_copy(i):
        return remote(near_out, near_in.at[i], ns.at[i], nr.at[i], {"ctx": partners[i]})

    def d_copy(h, i):
        return remote(dq_out.at[i, h], dq_in.at[i, h], ds.at[i, h], dr.at[i, h], {"ctx": partners[i]})

    listed = []
    for i in range(BITS):
        hit = jnp.float32(0.0)
        for slot in range(BITS):
            live = (blocks_ref[0, slot] == partners[i]) & (slot < count_ref[0])
            hit = jnp.where(live, 1.0, hit)
        listed.append(hit)
    off = [jnp.where(lower[i], 1.0 - listed[i], 0.0) for i in range(BITS)]

    gain_q = gain_q_ref[...]
    gain_k = gain_k_ref[...]

    def norm(raw, gain, hat, inv, normed, h):
        x = raw[h].astype(jnp.float32)
        inverse = lax.rsqrt(jnp.mean(x * x, axis=1, keepdims=True) + 1e-06)
        x_hat = x * inverse
        hat[h] = x_hat
        inv[h] = jnp.broadcast_to(inverse, x.shape)
        normed[h] = (x_hat * gain).astype(jnp.bfloat16)

    def norm_query(h):
        load(q_hbm, raw_q, 1, h).wait()
        load(g_hbm, gn, 0, h).wait()
        norm(raw_q, gain_q, q_hat, q_inv, qn, h)

    def send(h):
        if h == 0:
            pl.semaphore_wait(barrier, PEERS)
        for i in (0, 1):
            g_copy(h, i).start()
            q_copy(h, i).start()

    def load_kv(h):
        load(k_hbm, raw_k, 2, h).start()
        load(v_hbm, vn, 3, h).start()

    def norm_key(h):
        load(k_hbm, raw_k, 2, h).wait()
        load(v_hbm, vn, 3, h).wait()
        norm(raw_k, gain_k, k_hat, k_inv, kn, h)

    acc[...] = jnp.zeros_like(acc)

    def forward(h, slot, query, grad):
        scores = mm(kn[h], query, NT)
        largest = jnp.max(scores, axis=0, keepdims=True)
        e = jnp.exp2((scores - largest) * (FACTOR * LOG2E))
        total = jnp.sum(e, axis=0, keepdims=True)
        p = e * (1.0 / total)
        dp = mm(vn[h], grad, NT)
        prob[slot, h] = p
        dprob[slot, h] = dp
        dot = jnp.sum(p.astype(jnp.bfloat16).astype(jnp.float32) * dp, axis=0, keepdims=True)
        return largest * FACTOR + jnp.log(total), dot

    def far_forward(h):
        for i in (0, 1):
            g_copy(h, i).wait_recv()
            q_copy(h, i).wait_recv()
            log, dot = forward(h, i + 1, rq[i, h], rg[i, h])
            stat_out[h, i, 0:1] = jnp.where(off[i] > 0.5, FLOOR_LOG, log)
            stat_out[h, i, 1:2] = dot
            if i == 1:
                x_copy(h).start()
            s_copy(h, i).start()

    def near_forward(h):
        log, dot = forward(h, 0, qn[h], gn[h])
        near_out[h, 0:1] = log
        near_out[h, 1:2] = dot
        for i in range(BITS):
            near_out[h, 2 + i : 3 + i] = jnp.full((1, ROWS), off[i], jnp.float32)

    def send_near(h):
        for i in (1, 0):
            n_copy(i).start()

    def wait_near(h):
        for i in range(BITS):
            n_copy(i).wait_recv()

    def shares_of(logs, dots):
        top = jnp.maximum(jnp.maximum(logs[0], logs[1]), logs[2])
        parts = [jnp.exp(log - top) for log in logs]
        inverse = 1.0 / (parts[0] + parts[1] + parts[2])
        row_dot = (parts[0] * dots[0] + parts[1] * dots[1] + parts[2] * dots[2]) * inverse
        return parts[0] * inverse, row_dot

    def combine(h):
        logs = [near_out[h, 0:1]]
        dots = [near_out[h, 1:2]]
        for i in range(BITS):
            s_copy(h, i).wait_recv()
            logs.append(jnp.where(off[i] > 0.5, FLOOR_LOG, stat_in[h, i, 0:1]))
            dots.append(stat_in[h, i, 1:2])
        fin_own[h, 0:1], fin_own[h, 1:2] = shares_of(logs, dots)

    def far_shares(h, i):
        other = 1 - i
        logs = [
            jnp.where(near_in[i, h, 2 + i : 3 + i] > 0.5, FLOOR_LOG, stat_out[h, i, 0:1]),
            near_in[i, h, 0:1],
            jnp.where(near_in[i, h, 2 + other : 3 + other] > 0.5, FLOOR_LOG, cross_in[h, other, 0:1]),
        ]
        dots = [stat_out[h, i, 1:2], near_in[i, h, 1:2], cross_in[h, other, 1:2]]
        return shares_of(logs, dots)

    def one_back(h, slot, query, grad, share, row_dot):
        w = prob[slot, h] * share
        ds_t = (w * (dprob[slot, h] - row_dot) * FACTOR).astype(jnp.bfloat16)
        dk = mm(ds_t, query, NN)
        dq = mm(ds_t, kn[h], TN)
        return dq, dk

    def value_back(h, slot, grad, share):
        w = prob[slot, h] * share
        return mm(w.astype(jnp.bfloat16), grad, NN)

    def norm_back(hat, inv, gain, grad):
        gg = grad * gain
        inner = jnp.mean(hat * gg, axis=1, keepdims=True)
        return (inv * (gg - hat * inner)).astype(jnp.bfloat16)

    def fold(a):
        return jnp.sum(a.reshape(ROWS // 8, 8, HEAD_DIM), axis=0)

    def columns(h):
        return slice(h * HEAD_DIM, (h + 1) * HEAD_DIM)

    def store(src, dst, slot, h):
        return pltpu.make_async_copy(src.at[h], dst.at[:, columns(h)], store_sem.at[slot, h])

    def near_back(h):
        share = fin_own[h, 0:1]
        dq, dk = one_back(h, 0, qn[h], gn[h], share, fin_own[h, 1:2])
        dq_own[h] = dq
        dk_sum[h] = dk
        dv_sum[h] = value_back(h, 0, gn[h], share)
        acc[0] += fold(dq * q_hat[h])

    def far_back(h):
        gk = dk_sum[h]
        x_copy(h).wait_recv()
        for i in (1, 0):
            share, row_dot = far_shares(h, i)
            fin_far[h, i : i + 1] = share
            dq, dk = one_back(h, i + 1, rq[i, h], rg[i, h], share, row_dot)
            dq_out[i, h] = dq.astype(jnp.bfloat16)
            acc[1] += fold(dq * rq[i, h].astype(jnp.float32))
            gk = gk + dk
        dk_sum[h] = gk
        acc[2] += fold(gk * k_hat[h])

    def write_kv(h):
        gv = dv_sum[h]
        for i in range(BITS):
            gv = gv + value_back(h, i + 1, rg[i, h], fin_far[h, i : i + 1])
        ov[h] = gv.astype(jnp.bfloat16)
        store(ov, ov_hbm, 2, h).start()
        ok[h] = norm_back(k_hat[h], k_inv[h], gain_k, dk_sum[h])
        store(ok, ok_hbm, 1, h).start()

    def send_dq(h):
        for i in (1, 0):
            d_copy(h, i).start()

    def finish(h):
        for i in range(BITS):
            d_copy(h, i).wait_recv()
        gq = dq_own[h] + dq_in[0, h].astype(jnp.float32) + dq_in[1, h].astype(jnp.float32)
        oq[h] = norm_back(q_hat[h], q_inv[h], gain_q, gq)
        store(oq, oq_hbm, 0, h).start()

    def share_copies(buffer, index, peers, base):
        return [
            remote(buffer.at[index], buffer.at[index], as_.at[base + r], ar.at[base + r], peer)
            for r, peer in enumerate(peers)
        ]

    copies_a = share_copies(sum_a, column, head_peers, 0)
    copies_b = share_copies(sum_b, y, y_peers, HEAD_DEVS - 1)
    copies_c = share_copies(sum_c, z, z_peers, HEAD_DEVS + Y_DEVS - 2)

    def gain_sums(stage):
        if stage == 0:
            part_q = jnp.sum(acc[0], axis=0, keepdims=True)
            part_q += jnp.sum(acc[1], axis=0, keepdims=True) / gain_q
            sum_a[column, 0:1] = part_q
            sum_a[column, 1:2] = jnp.sum(acc[2], axis=0, keepdims=True)
            for c in copies_a:
                c.start()
        elif stage == 1:
            for c in copies_a:
                c.wait_recv()
            sum_b[y] = jnp.sum(sum_a[...], axis=0)
            for c in copies_b:
                c.start()
        elif stage == 2:
            for c in copies_a:
                c.wait_send()
            for c in copies_b:
                c.wait_recv()
            sum_c[z] = jnp.sum(sum_b[...], axis=0)
            for c in copies_c:
                c.start()
        else:
            for c in copies_b:
                c.wait_send()
            for c in copies_c:
                c.wait_recv()
            total = jnp.sum(sum_c[...], axis=0)
            ogain_ref[...] = total

    def wait_sent(h):
        for i in range(BITS):
            for copy in (q_copy, g_copy, s_copy, d_copy):
                copy(h, i).wait_send()
        x_copy(h).wait_send()
        if h == 0:
            for i in range(BITS):
                n_copy(i).wait_send()
        for slot, (src, dst) in enumerate(((oq, oq_hbm), (ok, ok_hbm), (ov, ov_hbm))):
            store(src, dst, slot, h).wait()

    steps = {
        "N": norm_query, "Q": send, "K": norm_key, "L": near_forward, "F": far_forward,
        "C": combine, "J": load_kv, "M": send_near, "V": wait_near, "G": near_back, "B": far_back, "H": write_kv, "W": wait_sent, "D": send_dq, "E": finish, "A": gain_sums,
    }
    for line in ORDER:
        for word in line.split():
            steps[word[0]](int(word[1]))

    for c in copies_c:
        c.wait_send()


def hand_over(q, k, v, gains, oq, ok, ov, ogain_q, ogain_k, sem):
    pairs = ((q, oq), (k, ok), (v, ov), (gains.at[0:1], ogain_q), (gains.at[1:2], ogain_k))
    copies = [pltpu.make_async_copy(src, dst, sem.at[n]) for n, (src, dst) in enumerate(pairs)]
    for c in copies:
        c.start()
    for c in copies:
        c.wait()


def body(q_raw, k_raw, values, grad_out, gain_q, gain_k, pair_blocks, pair_count):
    def vmem(*shape, dtype=jnp.float32):
        return pltpu.VMEM(shape, dtype)

    low = jnp.bfloat16
    tile = (HEADS, ROWS, HEAD_DIM)
    square = (BITS + 1, HEADS, ROWS, ROWS)
    wide = jax.ShapeDtypeStruct((ROWS, HEADS * HEAD_DIM), low)
    narrow = jax.ShapeDtypeStruct((1, HEAD_DIM), jnp.float32)
    any_space = pl.BlockSpec(memory_space=pl.ANY)
    in_vmem = pl.BlockSpec(memory_space=pltpu.VMEM)
    in_smem = pl.BlockSpec(memory_space=pltpu.SMEM)
    pair = pltpu.SemaphoreType.DMA((BITS, HEADS))
    parts = pl.pallas_call(
        kernel,
        out_shape=(pltpu.VMEM((ROWS, HEADS * HEAD_DIM), low),) * 3 + (pltpu.VMEM((2, HEAD_DIM), jnp.float32),),
        in_specs=[any_space] * 4 + [in_vmem] * 2 + [in_smem] * 2,
        out_specs=(any_space, any_space, any_space, in_vmem),
        scratch_shapes=[
            vmem(*tile, dtype=low), vmem(*tile, dtype=low),
            vmem(*tile, dtype=low), vmem(*tile, dtype=low), vmem(*tile, dtype=low), vmem(*tile, dtype=low),
            vmem(BITS, *tile, dtype=low), vmem(BITS, *tile, dtype=low),
            vmem(*tile), vmem(*tile), vmem(*tile), vmem(*tile),
            vmem(*square), vmem(*square),
            vmem(HEADS, 4, ROWS), vmem(BITS, HEADS, 4, ROWS),
            vmem(HEADS, BITS, 2, ROWS), vmem(HEADS, BITS, 2, ROWS), vmem(HEADS, BITS, 2, ROWS),
            vmem(HEADS, 2, ROWS), vmem(HEADS, BITS, ROWS),
            vmem(*tile), vmem(*tile), vmem(*tile), vmem(BITS, *tile, dtype=low), vmem(BITS, *tile, dtype=low),
            vmem(*tile, dtype=low), vmem(*tile, dtype=low), vmem(*tile, dtype=low),
            vmem(3, 8, HEAD_DIM),
            vmem(HEAD_DEVS, 2, HEAD_DIM), vmem(Y_DEVS, 2, HEAD_DIM), vmem(Z_DEVS, 2, HEAD_DIM),
            pltpu.SemaphoreType.DMA((4, HEADS)), pltpu.SemaphoreType.DMA((3, HEADS)),
            pair, pair, pair, pair, pair, pair,
            pltpu.SemaphoreType.DMA((BITS,)), pltpu.SemaphoreType.DMA((BITS,)),
            pltpu.SemaphoreType.DMA((HEADS,)), pltpu.SemaphoreType.DMA((HEADS,)), pair, pair,
            pltpu.SemaphoreType.DMA((PEERS,)), pltpu.SemaphoreType.DMA((PEERS,)),
        ],
        compiler_params=pltpu.CompilerParams(
            collective_id=0, has_side_effects=True, vmem_limit_bytes=56 * 1024 * 1024
        ),
        cost_estimate=pl.CostEstimate(
            flops=2 * 5 * 15 * ROWS * ROWS * HEAD_DIM,
            bytes_accessed=7 * ROWS * HEADS * HEAD_DIM * 2,
            transcendentals=15 * ROWS * ROWS,
        ),
    )(
        *[
            pltpu.with_memory_space_constraint(x, pltpu.HBM)
            for x in (q_raw, k_raw, values, grad_out, gain_q.reshape(1, HEAD_DIM), gain_k.reshape(1, HEAD_DIM))
        ],
        pair_blocks, pair_count,
    )
    grad_q, grad_k, grad_v, sum_q, sum_k = pl.pallas_call(
        hand_over,
        out_shape=(wide, wide, wide, narrow, narrow),
        in_specs=[any_space] * 4,
        out_specs=(any_space,) * 5,
        scratch_shapes=[pltpu.SemaphoreType.DMA((5,))],
        compiler_params=pltpu.CompilerParams(has_side_effects=True, vmem_limit_bytes=16 * 1024 * 1024),
    )(*parts)
    return grad_q, grad_k, grad_v, sum_q.reshape(HEAD_DIM), sum_k.reshape(HEAD_DIM)


def solution(mesh):
    placed = (
        P("ctx", "head"),
        P("ctx", "head"),
        P("ctx", "head"),
        P("ctx", "head"),
        P(),
        P(),
        P("ctx", None),
        P("ctx"),
    )
    return jax.shard_map(
        body,
        mesh=mesh,
        in_specs=placed,
        out_specs=(P("ctx", "head"), P("ctx", "head"), P("ctx", "head"), P(), P()),
        check_vma=False,
    )
```

```python
import math

import jax
import jax.numpy as jnp
from jax import lax
from jax.experimental import pallas as pl
from jax.experimental.pallas import tpu as pltpu
from jax.sharding import PartitionSpec as P

HEAD_DIM = 128
BITS = 2
ROWS = 256
HEADS = 5
FLOOR_LOG = -1e30
FACTOR = 1.0 / math.sqrt(HEAD_DIM)
LOG2E = 1.0 / math.log(2.0)
HEAD_DEVS = 8
Y_DEVS = 4
Z_DEVS = 8
PEERS = (HEAD_DEVS - 1) + (Y_DEVS - 1) + (Z_DEVS - 1)
MESH = pl.DeviceIdType.MESH
ORDER = (
    "N0 Q0 J0 J1",
    "J2 J3 J4 N1",
    "Q1 N2 N3 N4",
    "K0 K1 K2 K3",
    "K4 L0 L1 L2",
    "L3 L4 M0 F0",
    "Q2 F1 C0 Q3",
    "G0 F2 V0 B0",
    "C1 Q4 G1 B1",
    "F3 C2 G2 B2",
    "F4 D0 C3 G3",
    "B3 D1 C4 G4",
    "B4 A0 D2 H0",
    "H1 E0 A1 D3",
    "H2 H3 E1 W0",
    "W1 A2 D4 H4",
    "E2 W2 E3 W3",
    "E4 W4 A3",
)
NT = (((1,), (1,)), ((), ()))
NN = (((1,), (0,)), ((), ()))
TN = (((0,), (0,)), ((), ()))


def mm(a, b, dims):
    return lax.dot_general(a, b, dims, preferred_element_type=jnp.float32)


def kernel(
    q_hbm, k_hbm, v_hbm, g_hbm, gain_q_ref, gain_k_ref, blocks_ref, count_ref,
    oq_hbm, ok_hbm, ov_hbm, ogain_ref,
    raw_q, raw_k, qg, kn, vn, rqg,
    q_hat, q_inv, k_hat, k_inv, prob, dprob, near_out, near_in,
    stat_out, stat_in, cross_in, fin_own, fin_far, dq_own, dk_sum, dv_sum, dq_out, dq_in, oq, ok, ov, acc,
    sum_a, sum_b, sum_c,
    load_sem, store_sem, qs, qr, ss, sr, ns, nr, xs, xr, ds, dr, as_, ar,
):
    place = lax.axis_index("ctx")
    column = lax.axis_index("head")
    z = lax.rem(place, Z_DEVS)
    y = lax.div(place, Z_DEVS)
    partners = [jnp.bitwise_xor(place, 1 << i) for i in range(BITS)]
    across = {"ctx": jnp.bitwise_xor(place, 3)}
    lower = [jnp.bitwise_and(place, 1 << i) == 0 for i in range(BITS)]

    head_peers = [{"head": lax.rem(column + r, HEAD_DEVS)} for r in (4, 5, 3, 2, 6, 1, 7)]
    y_peers = [{"ctx": lax.rem(y + r, Y_DEVS) * Z_DEVS + z} for r in (2, 1, 3)]
    z_peers = [{"ctx": y * Z_DEVS + lax.rem(z + r, Z_DEVS)} for r in (4, 3, 5, 2, 6, 1, 7)]

    barrier = pltpu.get_barrier_semaphore()
    for peer in z_peers + y_peers + head_peers:
        pl.semaphore_signal(barrier, 1, device_id=peer, device_id_type=MESH)

    def load(src, dst, slot, h):
        return pltpu.make_async_copy(
            src.at[:, h * HEAD_DIM : (h + 1) * HEAD_DIM], dst.at[h], load_sem.at[slot, h]
        )

    def load_g(h):
        return pltpu.make_async_copy(
            g_hbm.at[:, h * HEAD_DIM : (h + 1) * HEAD_DIM], qg.at[h, 1], load_sem.at[0, h]
        )

    for h in range(HEADS):
        load_g(h).start()
        load(q_hbm, raw_q, 1, h).start()

    def remote(src, dst, send, recv, peer):
        return pltpu.make_async_remote_copy(
            src_ref=src, dst_ref=dst, send_sem=send, recv_sem=recv,
            device_id=peer, device_id_type=MESH,
        )

    def q_copy(h, i):
        return remote(qg.at[h], rqg.at[i, h], qs.at[i, h], qr.at[i, h], {"ctx": partners[i]})

    def s_copy(h, i):
        return remote(stat_out.at[h, i], stat_in.at[h, i], ss.at[i, h], sr.at[i, h], {"ctx": partners[i]})

    def x_copy(h):
        return remote(stat_out.at[h], cross_in.at[h], xs.at[h], xr.at[h], across)

    def n_copy(i):
        return remote(near_out, near_in.at[i], ns.at[i], nr.at[i], {"ctx": partners[i]})

    def d_copy(h, i):
        return remote(dq_out.at[i, h], dq_in.at[i, h], ds.at[i, h], dr.at[i, h], {"ctx": partners[i]})

    listed = []
    for i in range(BITS):
        hit = jnp.float32(0.0)
        for slot in range(BITS):
            live = (blocks_ref[0, slot] == partners[i]) & (slot < count_ref[0])
            hit = jnp.where(live, 1.0, hit)
        listed.append(hit)
    off = [jnp.where(lower[i], 1.0 - listed[i], 0.0) for i in range(BITS)]

    gain_q = gain_q_ref[...]
    gain_k = gain_k_ref[...]

    def norm(raw, gain, hat, inv, normed, h):
        x = raw[h].astype(jnp.float32)
        inverse = lax.rsqrt(jnp.mean(x * x, axis=1, keepdims=True) + 1e-06)
        x_hat = x * inverse
        hat[h] = x_hat
        inv[h] = jnp.broadcast_to(inverse, x.shape)
        if normed is qg:
            normed[h, 0] = (x_hat * gain).astype(jnp.bfloat16)
        else:
            normed[h] = (x_hat * gain).astype(jnp.bfloat16)

    def norm_query(h):
        load(q_hbm, raw_q, 1, h).wait()
        load_g(h).wait()
        norm(raw_q, gain_q, q_hat, q_inv, qg, h)

    def send(h):
        if h == 0:
            pl.semaphore_wait(barrier, PEERS)
        for i in (0, 1):
            q_copy(h, i).start()

    def load_kv(h):
        load(k_hbm, raw_k, 2, h).start()
        load(v_hbm, vn, 3, h).start()

    def norm_key(h):
        load(k_hbm, raw_k, 2, h).wait()
        load(v_hbm, vn, 3, h).wait()
        norm(raw_k, gain_k, k_hat, k_inv, kn, h)

    acc[...] = jnp.zeros_like(acc)

    def forward(h, slot, query, grad):
        scores = mm(kn[h], query, NT)
        largest = jnp.max(scores, axis=0, keepdims=True)
        e = jnp.exp2((scores - largest) * (FACTOR * LOG2E))
        total = jnp.sum(e, axis=0, keepdims=True)
        p = e * (1.0 / total)
        dp = mm(vn[h], grad, NT)
        prob[slot, h] = p
        dprob[slot, h] = dp
        dot = jnp.sum(p.astype(jnp.bfloat16).astype(jnp.float32) * dp, axis=0, keepdims=True)
        return largest * FACTOR + jnp.log(total), dot

    def far_forward(h):
        for i in (0, 1):
            q_copy(h, i).wait_recv()
            log, dot = forward(h, i + 1, rqg[i, h, 0], rqg[i, h, 1])
            stat_out[h, i, 0:1] = jnp.where(off[i] > 0.5, FLOOR_LOG, log)
            stat_out[h, i, 1:2] = dot
            if i == 1:
                x_copy(h).start()
            s_copy(h, i).start()

    def near_forward(h):
        log, dot = forward(h, 0, qg[h, 0], qg[h, 1])
        near_out[h, 0:1] = log
        near_out[h, 1:2] = dot
        for i in range(BITS):
            near_out[h, 2 + i : 3 + i] = jnp.full((1, ROWS), off[i], jnp.float32)

    def send_near(h):
        for i in (1, 0):
            n_copy(i).start()

    def wait_near(h):
        for i in range(BITS):
            n_copy(i).wait_recv()

    def shares_of(logs, dots):
        top = jnp.maximum(jnp.maximum(logs[0], logs[1]), logs[2])
        parts = [jnp.exp(log - top) for log in logs]
        inverse = 1.0 / (parts[0] + parts[1] + parts[2])
        row_dot = (parts[0] * dots[0] + parts[1] * dots[1] + parts[2] * dots[2]) * inverse
        return parts[0] * inverse, row_dot

    def combine(h):
        logs = [near_out[h, 0:1]]
        dots = [near_out[h, 1:2]]
        for i in range(BITS):
            s_copy(h, i).wait_recv()
            logs.append(jnp.where(off[i] > 0.5, FLOOR_LOG, stat_in[h, i, 0:1]))
            dots.append(stat_in[h, i, 1:2])
        fin_own[h, 0:1], fin_own[h, 1:2] = shares_of(logs, dots)

    def far_shares(h, i):
        other = 1 - i
        logs = [
            jnp.where(near_in[i, h, 2 + i : 3 + i] > 0.5, FLOOR_LOG, stat_out[h, i, 0:1]),
            near_in[i, h, 0:1],
            jnp.where(near_in[i, h, 2 + other : 3 + other] > 0.5, FLOOR_LOG, cross_in[h, other, 0:1]),
        ]
        dots = [stat_out[h, i, 1:2], near_in[i, h, 1:2], cross_in[h, other, 1:2]]
        return shares_of(logs, dots)

    def one_back(h, slot, query, grad, share, row_dot):
        w = prob[slot, h] * share
        ds_t = (w * (dprob[slot, h] - row_dot) * FACTOR).astype(jnp.bfloat16)
        dk = mm(ds_t, query, NN)
        dq = mm(ds_t, kn[h], TN)
        return dq, dk

    def value_back(h, slot, grad, share):
        w = prob[slot, h] * share
        return mm(w.astype(jnp.bfloat16), grad, NN)

    def norm_back(hat, inv, gain, grad):
        gg = grad * gain
        inner = jnp.mean(hat * gg, axis=1, keepdims=True)
        return (inv * (gg - hat * inner)).astype(jnp.bfloat16)

    def fold(a):
        return jnp.sum(a.reshape(ROWS // 8, 8, HEAD_DIM), axis=0)

    def columns(h):
        return slice(h * HEAD_DIM, (h + 1) * HEAD_DIM)

    def store(src, dst, slot, h):
        return pltpu.make_async_copy(src.at[h], dst.at[:, columns(h)], store_sem.at[slot, h])

    def near_back(h):
        share = fin_own[h, 0:1]
        dq, dk = one_back(h, 0, qg[h, 0], qg[h, 1], share, fin_own[h, 1:2])
        dq_own[h] = dq
        dk_sum[h] = dk
        dv_sum[h] = value_back(h, 0, qg[h, 1], share)
        acc[0] += fold(dq * q_hat[h])

    def far_back(h):
        gk = dk_sum[h]
        x_copy(h).wait_recv()
        for i in (1, 0):
            share, row_dot = far_shares(h, i)
            fin_far[h, i : i + 1] = share
            dq, dk = one_back(h, i + 1, rqg[i, h, 0], rqg[i, h, 1], share, row_dot)
            dq_out[i, h] = dq.astype(jnp.bfloat16)
            acc[1] += fold(dq * rqg[i, h, 0].astype(jnp.float32))
            gk = gk + dk
        dk_sum[h] = gk
        acc[2] += fold(gk * k_hat[h])

    def write_kv(h):
        gv = dv_sum[h]
        for i in range(BITS):
            gv = gv + value_back(h, i + 1, rqg[i, h, 1], fin_far[h, i : i + 1])
        ov[h] = gv.astype(jnp.bfloat16)
        store(ov, ov_hbm, 2, h).start()
        ok[h] = norm_back(k_hat[h], k_inv[h], gain_k, dk_sum[h])
        store(ok, ok_hbm, 1, h).start()

    def send_dq(h):
        for i in (1, 0):
            d_copy(h, i).start()

    def finish(h):
        for i in range(BITS):
            d_copy(h, i).wait_recv()
        gq = dq_own[h] + dq_in[0, h].astype(jnp.float32) + dq_in[1, h].astype(jnp.float32)
        oq[h] = norm_back(q_hat[h], q_inv[h], gain_q, gq)
        store(oq, oq_hbm, 0, h).start()

    def share_copies(buffer, index, peers, base):
        return [
            remote(buffer.at[index], buffer.at[index], as_.at[base + r], ar.at[base + r], peer)
            for r, peer in enumerate(peers)
        ]

    copies_a = share_copies(sum_a, column, head_peers, 0)
    copies_b = share_copies(sum_b, y, y_peers, HEAD_DEVS - 1)
    copies_c = share_copies(sum_c, z, z_peers, HEAD_DEVS + Y_DEVS - 2)

    def gain_sums(stage):
        if stage == 0:
            part_q = jnp.sum(acc[0], axis=0, keepdims=True)
            part_q += jnp.sum(acc[1], axis=0, keepdims=True) / gain_q
            sum_a[column, 0:1] = part_q
            sum_a[column, 1:2] = jnp.sum(acc[2], axis=0, keepdims=True)
            for c in copies_a:
                c.start()
        elif stage == 1:
            for c in copies_a:
                c.wait_recv()
            sum_b[y] = jnp.sum(sum_a[...], axis=0)
            for c in copies_b:
                c.start()
        elif stage == 2:
            for c in copies_a:
                c.wait_send()
            for c in copies_b:
                c.wait_recv()
            sum_c[z] = jnp.sum(sum_b[...], axis=0)
            for c in copies_c:
                c.start()
        else:
            for c in copies_b:
                c.wait_send()
            for c in copies_c:
                c.wait_recv()
            total = jnp.sum(sum_c[...], axis=0)
            ogain_ref[...] = total

    def wait_sent(h):
        for i in range(BITS):
            for copy in (q_copy, s_copy, d_copy):
                copy(h, i).wait_send()
        x_copy(h).wait_send()
        if h == 0:
            for i in range(BITS):
                n_copy(i).wait_send()
        for slot, (src, dst) in enumerate(((oq, oq_hbm), (ok, ok_hbm), (ov, ov_hbm))):
            store(src, dst, slot, h).wait()

    steps = {
        "N": norm_query, "Q": send, "K": norm_key, "L": near_forward, "F": far_forward,
        "C": combine, "J": load_kv, "M": send_near, "V": wait_near, "G": near_back, "B": far_back, "H": write_kv, "W": wait_sent, "D": send_dq, "E": finish, "A": gain_sums,
    }
    for line in ORDER:
        for word in line.split():
            steps[word[0]](int(word[1]))

    for c in copies_c:
        c.wait_send()


def hand_over(q, k, v, gains, oq, ok, ov, ogain_q, ogain_k, sem):
    pairs = ((q, oq), (k, ok), (v, ov), (gains.at[0:1], ogain_q), (gains.at[1:2], ogain_k))
    copies = [pltpu.make_async_copy(src, dst, sem.at[n]) for n, (src, dst) in enumerate(pairs)]
    for c in copies:
        c.start()
    for c in copies:
        c.wait()


def body(q_raw, k_raw, values, grad_out, gain_q, gain_k, pair_blocks, pair_count):
    def vmem(*shape, dtype=jnp.float32):
        return pltpu.VMEM(shape, dtype)

    low = jnp.bfloat16
    tile = (HEADS, ROWS, HEAD_DIM)
    square = (BITS + 1, HEADS, ROWS, ROWS)
    wide = jax.ShapeDtypeStruct((ROWS, HEADS * HEAD_DIM), low)
    narrow = jax.ShapeDtypeStruct((1, HEAD_DIM), jnp.float32)
    any_space = pl.BlockSpec(memory_space=pl.ANY)
    in_vmem = pl.BlockSpec(memory_space=pltpu.VMEM)
    in_smem = pl.BlockSpec(memory_space=pltpu.SMEM)
    pair = pltpu.SemaphoreType.DMA((BITS, HEADS))
    parts = pl.pallas_call(
        kernel,
        out_shape=(pltpu.VMEM((ROWS, HEADS * HEAD_DIM), low),) * 3 + (pltpu.VMEM((2, HEAD_DIM), jnp.float32),),
        in_specs=[any_space] * 4 + [in_vmem] * 2 + [in_smem] * 2,
        out_specs=(any_space, any_space, any_space, in_vmem),
        scratch_shapes=[
            vmem(*tile, dtype=low), vmem(*tile, dtype=low),
            vmem(HEADS, 2, ROWS, HEAD_DIM, dtype=low), vmem(*tile, dtype=low), vmem(*tile, dtype=low),
            vmem(BITS, HEADS, 2, ROWS, HEAD_DIM, dtype=low),
            vmem(*tile), vmem(*tile), vmem(*tile), vmem(*tile),
            vmem(*square), vmem(*square),
            vmem(HEADS, 4, ROWS), vmem(BITS, HEADS, 4, ROWS),
            vmem(HEADS, BITS, 2, ROWS), vmem(HEADS, BITS, 2, ROWS), vmem(HEADS, BITS, 2, ROWS),
            vmem(HEADS, 2, ROWS), vmem(HEADS, BITS, ROWS),
            vmem(*tile), vmem(*tile), vmem(*tile), vmem(BITS, *tile, dtype=low), vmem(BITS, *tile, dtype=low),
            vmem(*tile, dtype=low), vmem(*tile, dtype=low), vmem(*tile, dtype=low),
            vmem(3, 8, HEAD_DIM),
            vmem(HEAD_DEVS, 2, HEAD_DIM), vmem(Y_DEVS, 2, HEAD_DIM), vmem(Z_DEVS, 2, HEAD_DIM),
            pltpu.SemaphoreType.DMA((4, HEADS)), pltpu.SemaphoreType.DMA((3, HEADS)),
            pair, pair, pair, pair,
            pltpu.SemaphoreType.DMA((BITS,)), pltpu.SemaphoreType.DMA((BITS,)),
            pltpu.SemaphoreType.DMA((HEADS,)), pltpu.SemaphoreType.DMA((HEADS,)), pair, pair,
            pltpu.SemaphoreType.DMA((PEERS,)), pltpu.SemaphoreType.DMA((PEERS,)),
        ],
        compiler_params=pltpu.CompilerParams(
            collective_id=0, has_side_effects=True, vmem_limit_bytes=56 * 1024 * 1024
        ),
        cost_estimate=pl.CostEstimate(
            flops=2 * 5 * 15 * ROWS * ROWS * HEAD_DIM,
            bytes_accessed=7 * ROWS * HEADS * HEAD_DIM * 2,
            transcendentals=15 * ROWS * ROWS,
        ),
    )(
        *[
            pltpu.with_memory_space_constraint(x, pltpu.HBM)
            for x in (q_raw, k_raw, values, grad_out, gain_q.reshape(1, HEAD_DIM), gain_k.reshape(1, HEAD_DIM))
        ],
        pair_blocks, pair_count,
    )
    grad_q, grad_k, grad_v, sum_q, sum_k = pl.pallas_call(
        hand_over,
        out_shape=(wide, wide, wide, narrow, narrow),
        in_specs=[any_space] * 4,
        out_specs=(any_space,) * 5,
        scratch_shapes=[pltpu.SemaphoreType.DMA((5,))],
        compiler_params=pltpu.CompilerParams(has_side_effects=True, vmem_limit_bytes=16 * 1024 * 1024),
    )(*parts)
    return grad_q, grad_k, grad_v, sum_q.reshape(HEAD_DIM), sum_k.reshape(HEAD_DIM)


def solution(mesh):
    placed = (
        P("ctx", "head"),
        P("ctx", "head"),
        P("ctx", "head"),
        P("ctx", "head"),
        P(),
        P(),
        P("ctx", None),
        P("ctx"),
    )
    return jax.shard_map(
        body,
        mesh=mesh,
        in_specs=placed,
        out_specs=(P("ctx", "head"), P("ctx", "head"), P("ctx", "head"), P(), P()),
        check_vma=False,
    )
```

```python
import math

import jax
import jax.numpy as jnp
from jax import lax
from jax.experimental import pallas as pl
from jax.experimental.pallas import tpu as pltpu
from jax.sharding import PartitionSpec as P

HEAD_DIM = 128
BITS = 2
ROWS = 256
HEADS = 5
FLOOR_LOG = -1e30
FACTOR = 1.0 / math.sqrt(HEAD_DIM)
LOG2E = 1.0 / math.log(2.0)
HEAD_DEVS = 8
Y_DEVS = 4
Z_DEVS = 8
PEERS = (HEAD_DEVS - 1) + (Y_DEVS - 1) + (Z_DEVS - 1)
MESH = pl.DeviceIdType.MESH
ORDER = (
    "N0 Q0 J0 J1",
    "J2 J3 J4 N1",
    "Q1 N2 N3 N4",
    "K0 K1 K2 K3",
    "K4 L0 L1 L2",
    "L3 L4 M0 F0",
    "Q2 F1 C0 Q3",
    "G0 F2 V0 B0",
    "C1 Q4 G1 B1",
    "F3 C2 G2 B2",
    "F4 D0 C3 G3",
    "B3 D1 C4 G4",
    "B4 A0 D2 H0",
    "H1 E0 A1 D3",
    "H2 H3 E1 W0",
    "W1 A2 D4 H4",
    "E2 W2 E3 W3",
    "E4 W4 A3",
)
NT = (((1,), (1,)), ((), ()))
NN = (((1,), (0,)), ((), ()))
TN = (((0,), (0,)), ((), ()))


def mm(a, b, dims):
    return lax.dot_general(a, b, dims, preferred_element_type=jnp.float32)


def kernel(
    q_hbm, k_hbm, v_hbm, g_hbm, gain_q_ref, gain_k_ref, blocks_ref, count_ref,
    oq_hbm, ok_hbm, ov_hbm, ogain_ref,
    raw_q, raw_k, qn, kn, vn, gn, rq, rg,
    q_hat, q_inv, k_hat, k_inv, prob, dprob, near_out, near_in,
    stat_out, stat_in, cross_in, fin_own, fin_far, dq_own, dk_sum, dv_sum, dq_out, dq_in, oq, ok, ov, acc,
    sum_a, sum_b, sum_c,
    load_sem, store_sem, qs, qr, gs, gr, ss, sr, ns, nr, xs, xr, ds, dr, as_, ar,
):
    place = lax.axis_index("ctx")
    column = lax.axis_index("head")
    z = lax.rem(place, Z_DEVS)
    y = lax.div(place, Z_DEVS)
    partners = [jnp.bitwise_xor(place, 1 << i) for i in range(BITS)]
    across = {"ctx": jnp.bitwise_xor(place, 3)}
    lower = [jnp.bitwise_and(place, 1 << i) == 0 for i in range(BITS)]

    head_peers = [{"head": lax.rem(column + r, HEAD_DEVS)} for r in (4, 5, 3, 2, 6, 1, 7)]
    y_peers = [{"ctx": lax.rem(y + r, Y_DEVS) * Z_DEVS + z} for r in (2, 1, 3)]
    z_peers = [{"ctx": y * Z_DEVS + lax.rem(z + r, Z_DEVS)} for r in (4, 3, 5, 2, 6, 1, 7)]

    barrier = pltpu.get_barrier_semaphore()
    for peer in z_peers + y_peers + head_peers:
        pl.semaphore_signal(barrier, 1, device_id=peer, device_id_type=MESH)

    def load(src, dst, slot, h):
        return pltpu.make_async_copy(
            src.at[:, h * HEAD_DIM : (h + 1) * HEAD_DIM], dst.at[h], load_sem.at[slot, h]
        )

    for h in range(HEADS):
        load(g_hbm, gn, 0, h).start()
        load(q_hbm, raw_q, 1, h).start()

    def remote(src, dst, send, recv, peer):
        return pltpu.make_async_remote_copy(
            src_ref=src, dst_ref=dst, send_sem=send, recv_sem=recv,
            device_id=peer, device_id_type=MESH,
        )

    def q_copy(h, i):
        return remote(qn.at[h], rq.at[i, h], qs.at[i, h], qr.at[i, h], {"ctx": partners[i]})

    def g_copy(h, i):
        return remote(gn.at[h], rg.at[i, h], gs.at[i, h], gr.at[i, h], {"ctx": partners[i]})

    def s_copy(h, i):
        return remote(stat_out.at[h, i], stat_in.at[h, i], ss.at[i, h], sr.at[i, h], {"ctx": partners[i]})

    def x_copy(h):
        return remote(stat_out.at[h], cross_in.at[h], xs.at[h], xr.at[h], across)

    def n_copy(i):
        return remote(near_out, near_in.at[i], ns.at[i], nr.at[i], {"ctx": partners[i]})

    def d_copy(h, i):
        return remote(dq_out.at[i, h], dq_in.at[i, h], ds.at[i, h], dr.at[i, h], {"ctx": partners[i]})

    listed = []
    for i in range(BITS):
        hit = jnp.float32(0.0)
        for slot in range(BITS):
            live = (blocks_ref[0, slot] == partners[i]) & (slot < count_ref[0])
            hit = jnp.where(live, 1.0, hit)
        listed.append(hit)
    off = [jnp.where(lower[i], 1.0 - listed[i], 0.0) for i in range(BITS)]

    gain_q = gain_q_ref[...]
    gain_k = gain_k_ref[...]

    def norm(raw, gain, hat, inv, normed, h):
        x = raw[h].astype(jnp.float32)
        inverse = lax.rsqrt(jnp.mean(x * x, axis=1, keepdims=True) + 1e-06)
        x_hat = x * inverse
        hat[h] = x_hat
        inv[h] = jnp.broadcast_to(inverse, x.shape)
        normed[h] = (x_hat * gain).astype(jnp.bfloat16)

    def norm_query(h):
        if h == 0:
            load(g_hbm, gn, 0, h).wait()
            pl.semaphore_wait(barrier, PEERS)
            for i in (0, 1):
                g_copy(h, i).start()
        load(q_hbm, raw_q, 1, h).wait()
        if h > 0:
            load(g_hbm, gn, 0, h).wait()
        norm(raw_q, gain_q, q_hat, q_inv, qn, h)

    def send(h):
        for i in (0, 1):
            if h > 0:
                g_copy(h, i).start()
            q_copy(h, i).start()

    def load_kv(h):
        load(k_hbm, raw_k, 2, h).start()
        load(v_hbm, vn, 3, h).start()

    def norm_key(h):
        load(k_hbm, raw_k, 2, h).wait()
        load(v_hbm, vn, 3, h).wait()
        norm(raw_k, gain_k, k_hat, k_inv, kn, h)

    acc[...] = jnp.zeros_like(acc)

    def forward(h, slot, query, grad):
        scores = mm(kn[h], query, NT)
        largest = jnp.max(scores, axis=0, keepdims=True)
        e = jnp.exp2((scores - largest) * (FACTOR * LOG2E))
        total = jnp.sum(e, axis=0, keepdims=True)
        p = e * (1.0 / total)
        dp = mm(vn[h], grad, NT)
        prob[slot, h] = p
        dprob[slot, h] = dp
        dot = jnp.sum(p.astype(jnp.bfloat16).astype(jnp.float32) * dp, axis=0, keepdims=True)
        return largest * FACTOR + jnp.log(total), dot

    def far_forward(h):
        for i in (0, 1):
            g_copy(h, i).wait_recv()
            q_copy(h, i).wait_recv()
            log, dot = forward(h, i + 1, rq[i, h], rg[i, h])
            stat_out[h, i, 0:1] = jnp.where(off[i] > 0.5, FLOOR_LOG, log)
            stat_out[h, i, 1:2] = dot
            if i == 1:
                x_copy(h).start()
            s_copy(h, i).start()

    def near_forward(h):
        log, dot = forward(h, 0, qn[h], gn[h])
        near_out[h, 0:1] = log
        near_out[h, 1:2] = dot
        for i in range(BITS):
            near_out[h, 2 + i : 3 + i] = jnp.full((1, ROWS), off[i], jnp.float32)

    def send_near(h):
        for i in (1, 0):
            n_copy(i).start()

    def wait_near(h):
        for i in range(BITS):
            n_copy(i).wait_recv()

    def shares_of(logs, dots):
        top = jnp.maximum(jnp.maximum(logs[0], logs[1]), logs[2])
        parts = [jnp.exp(log - top) for log in logs]
        inverse = 1.0 / (parts[0] + parts[1] + parts[2])
        row_dot = (parts[0] * dots[0] + parts[1] * dots[1] + parts[2] * dots[2]) * inverse
        return parts[0] * inverse, row_dot

    def combine(h):
        logs = [near_out[h, 0:1]]
        dots = [near_out[h, 1:2]]
        for i in range(BITS):
            s_copy(h, i).wait_recv()
            logs.append(jnp.where(off[i] > 0.5, FLOOR_LOG, stat_in[h, i, 0:1]))
            dots.append(stat_in[h, i, 1:2])
        fin_own[h, 0:1], fin_own[h, 1:2] = shares_of(logs, dots)

    def far_shares(h, i):
        other = 1 - i
        logs = [
            jnp.where(near_in[i, h, 2 + i : 3 + i] > 0.5, FLOOR_LOG, stat_out[h, i, 0:1]),
            near_in[i, h, 0:1],
            jnp.where(near_in[i, h, 2 + other : 3 + other] > 0.5, FLOOR_LOG, cross_in[h, other, 0:1]),
        ]
        dots = [stat_out[h, i, 1:2], near_in[i, h, 1:2], cross_in[h, other, 1:2]]
        return shares_of(logs, dots)

    def one_back(h, slot, query, grad, share, row_dot):
        w = prob[slot, h] * share
        ds_t = (w * (dprob[slot, h] - row_dot) * FACTOR).astype(jnp.bfloat16)
        dk = mm(ds_t, query, NN)
        dq = mm(ds_t, kn[h], TN)
        return dq, dk

    def value_back(h, slot, grad, share):
        w = prob[slot, h] * share
        return mm(w.astype(jnp.bfloat16), grad, NN)

    def norm_back(hat, inv, gain, grad):
        gg = grad * gain
        inner = jnp.mean(hat * gg, axis=1, keepdims=True)
        return (inv * (gg - hat * inner)).astype(jnp.bfloat16)

    def fold(a):
        return jnp.sum(a.reshape(ROWS // 8, 8, HEAD_DIM), axis=0)

    def columns(h):
        return slice(h * HEAD_DIM, (h + 1) * HEAD_DIM)

    def store(src, dst, slot, h):
        return pltpu.make_async_copy(src.at[h], dst.at[:, columns(h)], store_sem.at[slot, h])

    def near_back(h):
        share = fin_own[h, 0:1]
        dq, dk = one_back(h, 0, qn[h], gn[h], share, fin_own[h, 1:2])
        dq_own[h] = dq
        dk_sum[h] = dk
        dv_sum[h] = value_back(h, 0, gn[h], share)
        acc[0] += fold(dq * q_hat[h])

    def far_back(h):
        gk = dk_sum[h]
        x_copy(h).wait_recv()
        for i in (1, 0):
            share, row_dot = far_shares(h, i)
            fin_far[h, i : i + 1] = share
            dq, dk = one_back(h, i + 1, rq[i, h], rg[i, h], share, row_dot)
            dq_out[i, h] = dq.astype(jnp.bfloat16)
            acc[1] += fold(dq * rq[i, h].astype(jnp.float32))
            gk = gk + dk
        dk_sum[h] = gk
        acc[2] += fold(gk * k_hat[h])

    def write_kv(h):
        gv = dv_sum[h]
        for i in range(BITS):
            gv = gv + value_back(h, i + 1, rg[i, h], fin_far[h, i : i + 1])
        ov[h] = gv.astype(jnp.bfloat16)
        store(ov, ov_hbm, 2, h).start()
        ok[h] = norm_back(k_hat[h], k_inv[h], gain_k, dk_sum[h])
        store(ok, ok_hbm, 1, h).start()

    def send_dq(h):
        for i in (1, 0):
            d_copy(h, i).start()

    def finish(h):
        for i in range(BITS):
            d_copy(h, i).wait_recv()
        gq = dq_own[h] + dq_in[0, h].astype(jnp.float32) + dq_in[1, h].astype(jnp.float32)
        oq[h] = norm_back(q_hat[h], q_inv[h], gain_q, gq)
        store(oq, oq_hbm, 0, h).start()

    def share_copies(buffer, index, peers, base):
        return [
            remote(buffer.at[index], buffer.at[index], as_.at[base + r], ar.at[base + r], peer)
            for r, peer in enumerate(peers)
        ]

    copies_a = share_copies(sum_a, column, head_peers, 0)
    copies_b = share_copies(sum_b, y, y_peers, HEAD_DEVS - 1)
    copies_c = share_copies(sum_c, z, z_peers, HEAD_DEVS + Y_DEVS - 2)

    def gain_sums(stage):
        if stage == 0:
            part_q = jnp.sum(acc[0], axis=0, keepdims=True)
            part_q += jnp.sum(acc[1], axis=0, keepdims=True) / gain_q
            sum_a[column, 0:1] = part_q
            sum_a[column, 1:2] = jnp.sum(acc[2], axis=0, keepdims=True)
            for c in copies_a:
                c.start()
        elif stage == 1:
            for c in copies_a:
                c.wait_recv()
            sum_b[y] = jnp.sum(sum_a[...], axis=0)
            for c in copies_b:
                c.start()
        elif stage == 2:
            for c in copies_a:
                c.wait_send()
            for c in copies_b:
                c.wait_recv()
            sum_c[z] = jnp.sum(sum_b[...], axis=0)
            for c in copies_c:
                c.start()
        else:
            for c in copies_b:
                c.wait_send()
            for c in copies_c:
                c.wait_recv()
            total = jnp.sum(sum_c[...], axis=0)
            ogain_ref[...] = total

    def wait_sent(h):
        for i in range(BITS):
            for copy in (q_copy, g_copy, s_copy, d_copy):
                copy(h, i).wait_send()
        x_copy(h).wait_send()
        if h == 0:
            for i in range(BITS):
                n_copy(i).wait_send()
        for slot, (src, dst) in enumerate(((oq, oq_hbm), (ok, ok_hbm), (ov, ov_hbm))):
            store(src, dst, slot, h).wait()

    steps = {
        "N": norm_query, "Q": send, "K": norm_key, "L": near_forward, "F": far_forward,
        "C": combine, "J": load_kv, "M": send_near, "V": wait_near, "G": near_back, "B": far_back, "H": write_kv, "W": wait_sent, "D": send_dq, "E": finish, "A": gain_sums,
    }
    for line in ORDER:
        for word in line.split():
            steps[word[0]](int(word[1]))

    for c in copies_c:
        c.wait_send()


def hand_over(q, k, v, gains, oq, ok, ov, ogain_q, ogain_k, sem):
    pairs = ((q, oq), (k, ok), (v, ov), (gains.at[0:1], ogain_q), (gains.at[1:2], ogain_k))
    copies = [pltpu.make_async_copy(src, dst, sem.at[n]) for n, (src, dst) in enumerate(pairs)]
    for c in copies:
        c.start()
    for c in copies:
        c.wait()


def body(q_raw, k_raw, values, grad_out, gain_q, gain_k, pair_blocks, pair_count):
    def vmem(*shape, dtype=jnp.float32):
        return pltpu.VMEM(shape, dtype)

    low = jnp.bfloat16
    tile = (HEADS, ROWS, HEAD_DIM)
    square = (BITS + 1, HEADS, ROWS, ROWS)
    wide = jax.ShapeDtypeStruct((ROWS, HEADS * HEAD_DIM), low)
    narrow = jax.ShapeDtypeStruct((1, HEAD_DIM), jnp.float32)
    any_space = pl.BlockSpec(memory_space=pl.ANY)
    in_vmem = pl.BlockSpec(memory_space=pltpu.VMEM)
    in_smem = pl.BlockSpec(memory_space=pltpu.SMEM)
    pair = pltpu.SemaphoreType.DMA((BITS, HEADS))
    parts = pl.pallas_call(
        kernel,
        out_shape=(pltpu.VMEM((ROWS, HEADS * HEAD_DIM), low),) * 3 + (pltpu.VMEM((2, HEAD_DIM), jnp.float32),),
        in_specs=[any_space] * 4 + [in_vmem] * 2 + [in_smem] * 2,
        out_specs=(any_space, any_space, any_space, in_vmem),
        scratch_shapes=[
            vmem(*tile, dtype=low), vmem(*tile, dtype=low),
            vmem(*tile, dtype=low), vmem(*tile, dtype=low), vmem(*tile, dtype=low), vmem(*tile, dtype=low),
            vmem(BITS, *tile, dtype=low), vmem(BITS, *tile, dtype=low),
            vmem(*tile), vmem(*tile), vmem(*tile), vmem(*tile),
            vmem(*square), vmem(*square),
            vmem(HEADS, 4, ROWS), vmem(BITS, HEADS, 4, ROWS),
            vmem(HEADS, BITS, 2, ROWS), vmem(HEADS, BITS, 2, ROWS), vmem(HEADS, BITS, 2, ROWS),
            vmem(HEADS, 2, ROWS), vmem(HEADS, BITS, ROWS),
            vmem(*tile), vmem(*tile), vmem(*tile), vmem(BITS, *tile, dtype=low), vmem(BITS, *tile, dtype=low),
            vmem(*tile, dtype=low), vmem(*tile, dtype=low), vmem(*tile, dtype=low),
            vmem(3, 8, HEAD_DIM),
            vmem(HEAD_DEVS, 2, HEAD_DIM), vmem(Y_DEVS, 2, HEAD_DIM), vmem(Z_DEVS, 2, HEAD_DIM),
            pltpu.SemaphoreType.DMA((4, HEADS)), pltpu.SemaphoreType.DMA((3, HEADS)),
            pair, pair, pair, pair, pair, pair,
            pltpu.SemaphoreType.DMA((BITS,)), pltpu.SemaphoreType.DMA((BITS,)),
            pltpu.SemaphoreType.DMA((HEADS,)), pltpu.SemaphoreType.DMA((HEADS,)), pair, pair,
            pltpu.SemaphoreType.DMA((PEERS,)), pltpu.SemaphoreType.DMA((PEERS,)),
        ],
        compiler_params=pltpu.CompilerParams(
            collective_id=0, has_side_effects=True, vmem_limit_bytes=56 * 1024 * 1024
        ),
        cost_estimate=pl.CostEstimate(
            flops=2 * 5 * 15 * ROWS * ROWS * HEAD_DIM,
            bytes_accessed=7 * ROWS * HEADS * HEAD_DIM * 2,
            transcendentals=15 * ROWS * ROWS,
        ),
    )(
        *[
            pltpu.with_memory_space_constraint(x, pltpu.HBM)
            for x in (q_raw, k_raw, values, grad_out, gain_q.reshape(1, HEAD_DIM), gain_k.reshape(1, HEAD_DIM))
        ],
        pair_blocks, pair_count,
    )
    grad_q, grad_k, grad_v, sum_q, sum_k = pl.pallas_call(
        hand_over,
        out_shape=(wide, wide, wide, narrow, narrow),
        in_specs=[any_space] * 4,
        out_specs=(any_space,) * 5,
        scratch_shapes=[pltpu.SemaphoreType.DMA((5,))],
        compiler_params=pltpu.CompilerParams(has_side_effects=True, vmem_limit_bytes=16 * 1024 * 1024),
    )(*parts)
    return grad_q, grad_k, grad_v, sum_q.reshape(HEAD_DIM), sum_k.reshape(HEAD_DIM)


def solution(mesh):
    placed = (
        P("ctx", "head"),
        P("ctx", "head"),
        P("ctx", "head"),
        P("ctx", "head"),
        P(),
        P(),
        P("ctx", None),
        P("ctx"),
    )
    return jax.shard_map(
        body,
        mesh=mesh,
        in_specs=placed,
        out_specs=(P("ctx", "head"), P("ctx", "head"), P("ctx", "head"), P(), P()),
        check_vma=False,
    )
```
